256 devices in a mesh: tm: 16 (over z, core), rows: 16 (over x, y).
Axes of the slice: x: 4, y: 4, z: 8, core: 2. Of those that a mesh axis runs over, the one named last changes fastest.
Arguments:
- frames_in: bfloat16 [16, 13312, 1152], P('tm', 'rows'), may hold values from -6 to 6
- norm_gain: bfloat16 [1152], replicated, may hold values from 0.5 to 1.5
- w_qkv: bfloat16 [1152, 3456], replicated, may hold values from -0.1875 to 0.1875
- out_gain: bfloat16 [1152], replicated, may hold values from 0.5 to 1.5
- w_out: bfloat16 [1152, 1152], replicated, may hold values from -0.1875 to 0.1875
Outputs:
- mixed_out: bfloat16 [16, 13312, 1152], P('tm', 'rows')
The draws below stay inside these ranges and needn't reach their ends.
All inputs are finite; a program needn't handle non-finite values.
Results may differ from the reference program's by a relative error of at most 0.0055.
Values sent between devices are 32-bit elements; how exact they have to be, the bound alone decides.
A program may use at most 64 MiB of HBM per device.

```python
import jax
import jax.numpy as jnp
from jax import lax

D = 1152
HEADS = 36
HEAD_DIM = 32
FRAMES = 16
FRAME_ROWS = 13312


def block_levels(key, extent, pieces, least, top_value):
    loudness, own = 1.0, jax.random.fold_in(key, 6)
    for axis_at, parts in pieces:
        draws = jnp.exp(jax.random.uniform(jax.random.fold_in(own, axis_at), (parts,), jnp.float32, least / len(pieces), top_value / len(pieces)))
        loudness = loudness * jnp.repeat(draws, extent[axis_at] // parts).reshape([-1 if axis == axis_at else 1 for axis in range(len(extent))])
    return loudness


def centred(own_key, extent, deviation, bound, pieces=(), kind=jnp.bfloat16):
    drawn = jax.random.normal(own_key, extent, jnp.float32) * deviation
    if len(pieces) > 0:
        drawn = block_levels(own_key, extent, pieces, -0.22, 0.18) * drawn
    return jnp.clip(drawn, min=-bound, max=bound).astype(kind)


def setup_inputs(seed: int = 0) -> dict:
    seeds = jax.random.split(jax.random.key(seed), 6)
    frames_in = centred(seeds[0], (FRAMES, FRAME_ROWS, D), 1.0, 6.0, ((0, 16), (1, 16)))
    norm_gain = jnp.clip(1.0 + 0.1 * jax.random.normal(seeds[1], (D,), jnp.float32), 0.5, 1.5).astype(jnp.bfloat16)
    w_qkv = centred(seeds[2], (D, 3 * D), D ** -0.5, 0.1875)
    out_gain = jnp.clip(1.0 + 0.1 * jax.random.normal(seeds[3], (D,), jnp.float32), 0.5, 1.5).astype(jnp.bfloat16)
    w_out = centred(seeds[4], (D, D), D ** -0.5, 0.1875)
    return dict(frames_in=frames_in, norm_gain=norm_gain, w_qkv=w_qkv, out_gain=out_gain, w_out=w_out)


EPSILON = 1e-06

def normalize(activations, gain_vec):
    floated = activations.astype(jnp.float32)
    inverse_rms = lax.rsqrt(lax.optimization_barrier(jnp.mean(floated * floated, axis=-1, keepdims=True)) + EPSILON)
    return floated * inverse_rms * gain_vec.astype(jnp.float32)

def reference(frames_in, norm_gain, w_qkv, out_gain, w_out):

    def frame_step(carried, frame_rows):
        row_count = frame_rows.shape[0]
        normed = normalize(frame_rows, norm_gain).astype(jnp.bfloat16)
        projected = jnp.dot(normed, w_qkv, preferred_element_type=jnp.float32)
        queries = jax.nn.relu(projected[:, :D]).astype(jnp.bfloat16)
        key_feats = jax.nn.relu(projected[:, D:2 * D]).astype(jnp.bfloat16)
        value_feats = projected[:, 2 * D:].astype(jnp.bfloat16)
        key_heads = key_feats.astype(jnp.float32).reshape(row_count, HEADS, HEAD_DIM)
        value_heads = value_feats.astype(jnp.float32).reshape(row_count, HEADS, HEAD_DIM)
        frame_state = jnp.einsum('rhe,rhf->ehf', key_heads, value_heads, precision=lax.Precision.HIGHEST)
        causal_state = carried + frame_state
        query_heads = queries.astype(jnp.float32).reshape(row_count, HEADS, HEAD_DIM)
        linear = jnp.einsum('rhe,ehf->rhf', query_heads, causal_state, precision=lax.Precision.HIGHEST).reshape(row_count, D)
        attended = normalize(linear, out_gain).astype(jnp.bfloat16)
        mixed_out = (frame_rows.astype(jnp.float32) + jnp.dot(attended, w_out, preferred_element_type=jnp.float32)).astype(jnp.bfloat16)
        return (causal_state, mixed_out)
    start_state = jnp.zeros((HEAD_DIM, HEADS, HEAD_DIM), jnp.float32)
    _, outputs = lax.scan(frame_step, start_state, frames_in)
    return outputs
```

```python
import functools

import jax
import jax.numpy as jnp
from jax import lax
from jax.experimental import pallas as pl
from jax.experimental.pallas import tpu as pltpu
from jax.sharding import PartitionSpec as P

HEAD_DIM = 32
EPSILON = 1e-06
BLOCK = 128
CHUNK = 256
GROUPS = ((0, 6), (6, 9))
PEERS = 16
F32, BF16 = jnp.float32, jnp.bfloat16


def tile_rows(group):
    return -(-2 * (group[1] - group[0]) // 8) * 8


def chunks_of(start, stop):
    return [(at, min(CHUNK, stop - at)) for at in range(start, stop, CHUNK)]


def kernel(
    comm,
    x_hbm, norm_gain, wqkv_hbm, out_gain, wout_hbm, out_hbm,
    x_v, xg_v, w_v, wq_v, wo_v, kv_v, q_v, lin_v, acc_v, out_v, r2_v, ssq_v, state_v,
    x_sem, w_sem, wq_sem, wo_sem, out_sem, *exchange,
):
    rows, width = x_v.shape
    n_groups = len(GROUPS)
    sends, parts, owns, shares, wholes = (exchange[i * n_groups : (i + 1) * n_groups] for i in range(5))
    s1, r1, s2, r2, s3, r3 = exchange[5 * n_groups :]
    frame, band = (lax.axis_index("tm"), lax.axis_index("rows")) if comm else (0, 0)

    x_copy = pltpu.make_async_copy(x_hbm.at[0], x_v, x_sem)
    x_copy.start()
    w_copies = []
    for g, (first, last) in enumerate(GROUPS):
        wide = (last - first) * BLOCK
        for half in range(2):
            src = wqkv_hbm.at[:, pl.ds((half + 1) * width + first * BLOCK, wide)]
            dst = w_v.at[:, pl.ds(2 * first * BLOCK + half * wide, wide)]
            copy = pltpu.make_async_copy(src, dst, w_sem.at[g, half])
            copy.start()
            w_copies.append(copy)
    wq_copy = pltpu.make_async_copy(wqkv_hbm.at[:, pl.ds(0, width)], wq_v, wq_sem)
    wq_copy.start()
    wo_copy = pltpu.make_async_copy(wout_hbm, wo_v, wo_sem)
    wo_copy.start()

    if comm:
        barrier = pltpu.get_barrier_semaphore()
        for k in range(1, PEERS):
            pl.semaphore_signal(barrier, inc=1, device_id={"rows": lax.rem(band + k, PEERS)}, device_id_type=pl.DeviceIdType.MESH)
            pl.semaphore_signal(barrier, inc=1, device_id={"tm": lax.rem(frame + k, PEERS)}, device_id_type=pl.DeviceIdType.MESH)

    def mesh_copy(src, dst, send_sem, recv_sem, where):
        return pltpu.make_async_remote_copy(
            src_ref=src, dst_ref=dst, send_sem=send_sem, recv_sem=recv_sem,
            device_id=where, device_id_type=pl.DeviceIdType.MESH,
        )

    def slot(buf, index, g):
        deep = tile_rows(GROUPS[g])
        return buf.at[pl.ds(pl.multiple_of(index * deep, 8), deep)]

    def send_parts(g):
        if not comm:
            return
        for k in range(1, PEERS):
            to = lax.rem(band + k, PEERS)
            mesh_copy(slot(sends[g], to, g), slot(parts[g], k - 1, g), s1.at[g], r1.at[g], {"rows": to}).start()

    def bulk(buf, g):
        return buf.at[pl.ds(0, (PEERS - 1) * tile_rows(GROUPS[g]))]

    def send_share(g):
        if not comm:
            owns[g][...] = slot(sends[g], 0, g)[...]
            return
        mesh_copy(bulk(sends[g], g), bulk(parts[g], g), s1.at[g], r1.at[g], {"rows": band}).wait_recv()
        total = slot(sends[g], band, g)[...]
        for k in range(PEERS - 1):
            total += slot(parts[g], k, g)[...]
        owns[g][...] = total

        def send(to, _):
            mesh_copy(owns[g], slot(shares[g], frame, g), s2.at[g, to], r2.at[g, frame], {"tm": to}).start()
            return _

        lax.fori_loop(frame + 1, PEERS, send, 0)

    def send_causal(g):
        if not comm:
            wholes[g][...] = sends[g][...]
            return

        def arrived(i, _):
            mesh_copy(owns[g], slot(shares[g], i, g), s2.at[g, i], r2.at[g, i], {"tm": i}).wait_recv()
            return _

        lax.fori_loop(0, frame, arrived, 0)
        total = lax.fori_loop(0, frame, lambda i, t: t + slot(shares[g], i, g)[...], owns[g][...])
        mine = slot(wholes[g], band, g)
        mine[...] = total
        for k in range(1, PEERS):
            mesh_copy(mine, mine, s3.at[g], r3.at[g], {"rows": lax.rem(band + k, PEERS)}).start()

    def receive_causal(g):
        if comm:
            mesh_copy(bulk(wholes[g], g), bulk(wholes[g], g), s3.at[g], r3.at[g], {"rows": band}).wait_recv()

    def all_sent(g):
        if not comm:
            return
        mesh_copy(bulk(sends[g], g), bulk(parts[g], g), s1.at[g], r1.at[g], {"rows": band}).wait_send()
        mesh_copy(bulk(wholes[g], g), bulk(wholes[g], g), s3.at[g], r3.at[g], {"rows": band}).wait_send()

        def gone(to, _):
            mesh_copy(owns[g], slot(shares[g], frame, g), s2.at[g, to], r2.at[g, frame], {"tm": to}).wait_send()
            return _

        lax.fori_loop(frame + 1, PEERS, gone, 0)

    lane_head = lax.broadcasted_iota(jnp.int32, (HEAD_DIM, BLOCK), 1) // HEAD_DIM

    def project(g):
        first, last = GROUPS[g]
        base, wide = 2 * first * BLOCK, (last - first) * BLOCK
        w_copies[2 * g].wait()
        for at, size in chunks_of(0, 2 * wide):
            if at <= wide < at + size:
                w_copies[2 * g + 1].wait()
            done = jnp.dot(xg_v[...], w_v[:, base + at : base + at + size], preferred_element_type=F32)
            for col in range(0, size, BLOCK):
                piece = done[:, col : col + BLOCK]
                if at + col < wide:
                    piece = jnp.maximum(piece, 0.0) * r2_v[...]
                kv_v[:, base + at + col : base + at + col + BLOCK] = piece.astype(BF16)
        for at, size in chunks_of(0, wide):
            outer = lax.dot_general(
                kv_v[:, base + at : base + at + size], kv_v[:, base + wide + at : base + wide + at + size],
                (((0,), (0,)), ((), ())), preferred_element_type=F32,
            )
            for col in range(0, size, BLOCK):
                block = outer[col : col + BLOCK, col : col + BLOCK]
                state = jnp.where(lane_head == 0, block[:HEAD_DIM], 0.0)
                for a in range(1, BLOCK // HEAD_DIM):
                    state += jnp.where(lane_head == a, block[a * HEAD_DIM : (a + 1) * HEAD_DIM], 0.0)
                j, deep = (at + col) // BLOCK, tile_rows(GROUPS[g])
                for half in range(2):
                    sends[g][pl.ds(2 * j + half, PEERS, stride=deep), :] = state[half * PEERS : (half + 1) * PEERS]

    def attend(g):
        first, last = GROUPS[g]
        deep = tile_rows(GROUPS[g])
        for at, size in chunks_of(first * BLOCK, last * BLOCK):
            if size == CHUNK:
                state_v[...] = jnp.zeros_like(state_v)
            for col in range(0, size, BLOCK):
                j = (at + col) // BLOCK - first
                state = jnp.concatenate([wholes[g][pl.ds(2 * j + half, PEERS, stride=deep), :] for half in range(2)], axis=0)
                for a in range(BLOCK // HEAD_DIM):
                    state_v[col + a * HEAD_DIM : col + (a + 1) * HEAD_DIM, col : col + BLOCK] = jnp.where(
                        lane_head == a, state, 0.0
                    ).astype(BF16)
            linear = jnp.dot(q_v[:, at : at + size], state_v[:size, :size], preferred_element_type=F32)
            squares = linear * linear
            squares = squares[:, :BLOCK] + squares[:, BLOCK:] if size == CHUNK else squares
            ssq_v[...] = squares if at == 0 else ssq_v[...] + squares
            gain = out_gain[at : at + size].astype(F32)
            lin_v[:, at : at + size] = (linear * gain).astype(BF16)

    def mix(g):
        first, last = GROUPS[g]
        rows_of = slice(first * BLOCK, last * BLOCK)
        for at, size in chunks_of(0, width):
            done = jnp.dot(lin_v[:, rows_of], wo_v[rows_of, at : at + size], preferred_element_type=F32)
            acc_v[:, at : at + size] = done if g == 0 else acc_v[:, at : at + size] + done

    def finish(g):
        first, last = GROUPS[g]
        rows_of = slice(first * BLOCK, last * BLOCK)
        ssq = jnp.sum(ssq_v[...], axis=1, keepdims=True) / width
        factor2 = r2_v[...]
        scale = jnp.sqrt(factor2) * lax.rsqrt(factor2 * ssq + EPSILON)
        r2_v[...] = scale
        copies = []
        for at, size in chunks_of(0, width):
            done = jnp.dot(lin_v[:, rows_of], wo_v[rows_of, at : at + size], preferred_element_type=F32)
            for col in range(0, size, BLOCK):
                here = slice(at + col, at + col + BLOCK)
                piece = (acc_v[:, here] + done[:, col : col + BLOCK]) * r2_v[...]
                out_v[:, here] = (x_v[:, here].astype(F32) + piece).astype(BF16)
            copy = pltpu.make_async_copy(
                out_v.at[:, pl.ds(at, size)], out_hbm.at[0, :, pl.ds(at, size)], out_sem.at[at // CHUNK]
            )
            copy.start()
            copies.append(copy)
        for copy in copies:
            copy.wait()

    x_copy.wait()
    total = jnp.zeros((rows, BLOCK), F32)
    for col in range(0, width, BLOCK):
        piece = x_v[:, col : col + BLOCK].astype(F32)
        total += piece * piece
        xg_v[:, col : col + BLOCK] = (piece * norm_gain[col : col + BLOCK].astype(F32)).astype(BF16)
    mean = jnp.sum(total, axis=1, keepdims=True) / width
    r2_v[...] = jnp.broadcast_to(1.0 / (mean + EPSILON), (rows, BLOCK))

    project(0)
    if comm:
        pl.semaphore_wait(barrier, 2 * (PEERS - 1))
    send_parts(0)
    project(1)
    send_parts(1)
    send_share(0)
    wq_copy.wait()
    q_chunks = chunks_of(0, width)
    for i, (at, size) in enumerate(q_chunks):
        done = jnp.dot(xg_v[...], wq_v[:, at : at + size], preferred_element_type=F32)
        q_v[:, at : at + size] = jnp.maximum(done, 0.0).astype(BF16)
        if i == 1:
            send_causal(0)
        if i == 2:
            send_share(1)
    receive_causal(0)
    attend(0)
    send_causal(1)
    wo_copy.wait()
    mix(0)
    receive_causal(1)
    attend(1)
    finish(1)
    for g in range(n_groups):
        all_sent(g)


def make_call(rows, width, comm=True):
    n_groups = len(GROUPS)
    vm = pltpu.VMEM
    deeps = [tile_rows(g) for g in GROUPS]
    dma = pltpu.SemaphoreType.DMA
    whole = [vm((PEERS * d, BLOCK), F32) for d in deeps]
    scratch = [
        vm((rows, width), BF16),
        vm((rows, width), BF16),
        vm((width, 2 * width), BF16),
        vm((width, width), BF16),
        vm((width, width), BF16),
        vm((rows, 2 * width), BF16),
        vm((rows, width), BF16),
        vm((rows, width), BF16),
        vm((rows, width), F32),
        vm((rows, width), BF16),
        vm((rows, BLOCK), F32),
        vm((rows, BLOCK), F32),
        vm((CHUNK, CHUNK), BF16),
        dma, dma((n_groups, 2)), dma, dma, dma((-(-width // CHUNK),)),
        *whole, *whole, *[vm((d, BLOCK), F32) for d in deeps], *whole, *whole,
        dma((n_groups,)), dma((n_groups,)), dma((n_groups, PEERS)), dma((n_groups, PEERS)), dma((n_groups,)), dma((n_groups,)),
    ]
    hbm = pl.BlockSpec(memory_space=pltpu.HBM)
    vec = pl.BlockSpec(memory_space=pltpu.VMEM)
    return pl.pallas_call(
        functools.partial(kernel, comm),
        out_shape=jax.ShapeDtypeStruct((1, rows, width), BF16),
        in_specs=[hbm, vec, hbm, vec, hbm],
        out_specs=hbm,
        scratch_shapes=scratch,
        compiler_params=pltpu.CompilerParams(
            collective_id=0 if comm else None, has_side_effects=comm, vmem_limit_bytes=60 * 2**20
        ),
        cost_estimate=pl.CostEstimate(flops=10**10, bytes_accessed=15 * 10**6, transcendentals=0),
    )


def body(frames_in, norm_gain, w_qkv, out_gain, w_out):
    call = make_call(frames_in.shape[1], frames_in.shape[2])
    return call(frames_in, norm_gain, w_qkv, out_gain, w_out)


def solution(mesh):
    in_specs = (P("tm", "rows", None), P(), P(), P(), P())
    out_specs = P("tm", "rows", None)
    return jax.shard_map(body, mesh=mesh, in_specs=in_specs, out_specs=out_specs, check_vma=False)
```

```python
import functools

import jax
import jax.numpy as jnp
from jax import lax
from jax.experimental import pallas as pl
from jax.experimental.pallas import tpu as pltpu
from jax.sharding import PartitionSpec as P

HEAD_DIM = 32
EPSILON = 1e-06
BLOCK = 128
CHUNK = 256
GROUPS = ((0, 6), (6, 9))
DEEP = 16
PEERS = 16
SIDE = 4
F32, BF16 = jnp.float32, jnp.bfloat16
MESH = pl.DeviceIdType.MESH
AWAY = sorted(
    ((dx, dy) for dx in range(SIDE) for dy in range(SIDE) if dx or dy),
    key=lambda d: -sum(min(a, SIDE - a) for a in d),
)


def chunks_of(start, stop):
    return [(at, min(CHUNK, stop - at)) for at in range(start, stop, CHUNK)]


def kernel(
    comm,
    x_hbm, norm_gain, wqkv_hbm, out_gain, wout_hbm, out_v,
    x_v, xg_v, w_v, wq_v, wo_v, kv_v, q_v, lin_v, acc_v, r2_v, ssq_v,
    sends, parts, owns, shares, wholes,
    x_sem, w_sem, wq_sem, wo_sem, s1, r1, s2, r2, s3, r3,
):
    rows, width = x_v.shape
    n_groups = len(GROUPS)
    frame, band = (lax.axis_index("tm"), lax.axis_index("rows")) if comm else (0, 0)

    x_copy = pltpu.make_async_copy(x_hbm.at[0], x_v, x_sem)
    x_copy.start()
    w_copies = []
    for g, (first, last) in enumerate(GROUPS):
        wide = (last - first) * BLOCK
        pair = []
        for half in range(2):
            src = wqkv_hbm.at[:, pl.ds((2 - half) * width + first * BLOCK, wide)]
            dst = w_v.at[:, pl.ds(2 * first * BLOCK + half * wide, wide)]
            pair.append(pltpu.make_async_copy(src, dst, w_sem.at[g, half]))
            pair[-1].start()
        w_copies.append(pair)
    wq_copy = pltpu.make_async_copy(wqkv_hbm.at[:, pl.ds(0, width)], wq_v, wq_sem)
    wo_copy = pltpu.make_async_copy(wout_hbm, wo_v, wo_sem)

    if comm:
        barrier = pltpu.get_barrier_semaphore()

        def greet(k, _):
            pl.semaphore_signal(barrier, inc=1, device_id={"rows": lax.rem(band + k, PEERS)}, device_id_type=MESH)
            pl.semaphore_signal(barrier, inc=1, device_id={"tm": lax.rem(frame + k, PEERS)}, device_id_type=MESH)
            return _

        lax.fori_loop(1, PEERS, greet, 0)

    others = [lax.rem(band // SIDE + dx, SIDE) * SIDE + lax.rem(band + dy, SIDE) for dx, dy in AWAY]

    def mesh_copy(src, dst, send_sem, recv_sem, where):
        return pltpu.make_async_remote_copy(
            src_ref=src, dst_ref=dst, send_sem=send_sem, recv_sem=recv_sem, device_id=where, device_id_type=MESH
        )

    def slot(buf, g, index):
        return buf.at[g, pl.ds(pl.multiple_of(index * DEEP, 8), DEEP)]

    def bulk(buf, g):
        return buf.at[g, pl.ds(0, (PEERS - 1) * DEEP)]

    def part_copies(g):
        return mesh_copy(bulk(sends, g), bulk(parts, g), s1.at[g], r1.at[g], {"rows": band})

    def share_copy(g, source, to):
        return mesh_copy(owns.at[g], slot(shares, g, source), s2.at[g, to], r2.at[g, source], {"tm": to})

    def whole_copies(g):
        return mesh_copy(bulk(wholes, g), bulk(wholes, g), s3.at[g], r3.at[g], {"rows": band})

    def send_parts(g):
        if comm:
            for k, to in enumerate(others):
                mesh_copy(slot(sends, g, to), slot(parts, g, k), s1.at[g], r1.at[g], {"rows": to}).start()

    def send_share(g):
        part_copies(g).wait_recv()
        total = slot(sends, g, band)[...]
        for k in range(PEERS - 1):
            total += slot(parts, g, k)[...]
        owns[g] = total

        def send(to, _):
            share_copy(g, frame, to).start()
            return _

        lax.fori_loop(frame + 1, PEERS, send, 0)

    def send_causal(g):
        def arrived(i, _):
            share_copy(g, i, i).wait_recv()
            return _

        lax.fori_loop(0, frame, arrived, 0)
        total = owns[g]
        for i in range(PEERS - 1):
            total += jnp.where(i < frame, slot(shares, g, i)[...], 0.0)
        mine = slot(wholes, g, band)
        mine[...] = total
        for to in others:
            mesh_copy(mine, mine, s3.at[g], r3.at[g], {"rows": to}).start()

    def each_group(step):
        def one(g, _):
            step(g)
            return _

        lax.fori_loop(0, n_groups, one, 0)

    def sent(g):
        part_copies(g).wait_send()

        def gone(to, _):
            share_copy(g, frame, to).wait_send()
            return _

        lax.fori_loop(frame + 1, PEERS, gone, 0)
        whole_copies(g).wait_send()

    lane_head = lax.broadcasted_iota(jnp.int32, (HEAD_DIM, BLOCK), 1) // HEAD_DIM

    def project(g):
        first, last = GROUPS[g]
        base, wide = 2 * first * BLOCK, (last - first) * BLOCK
        for at, size in chunks_of(base, base + 2 * wide):
            done = jnp.dot(xg_v[...], w_v[:, at : at + size], preferred_element_type=F32)
            for col in range(at, at + size, BLOCK):
                piece = done[:, col - at : col - at + BLOCK]
                if col >= base + wide:
                    piece = jnp.maximum(piece, 0.0) * r2_v[...]
                kv_v[:, col : col + BLOCK] = piece.astype(BF16)
        for j in range(last - first):
            at = base + j * BLOCK
            block = lax.dot_general(
                kv_v[:, at + wide : at + wide + BLOCK], kv_v[:, at : at + BLOCK],
                (((0,), (0,)), ((), ())), preferred_element_type=F32,
            )
            state = jnp.where(lane_head == 0, block[:HEAD_DIM], 0.0)
            for a in range(1, BLOCK // HEAD_DIM):
                state += jnp.where(lane_head == a, block[a * HEAD_DIM : (a + 1) * HEAD_DIM], 0.0)
            for half in range(2):
                sends[g, pl.ds(2 * j + half, PEERS, stride=DEEP), :] = state[half * PEERS : (half + 1) * PEERS]

    def attend(g):
        first, last = GROUPS[g]
        whole = wholes if comm else sends
        zeros = jnp.zeros((BLOCK, BLOCK), BF16)
        for at, size in chunks_of(first * BLOCK, last * BLOCK):
            blocks = []
            for col in range(at, at + size, BLOCK):
                j = col // BLOCK - first
                state = jnp.concatenate([whole[g, pl.ds(2 * j + half, PEERS, stride=DEEP), :] for half in range(2)], axis=0)
                heads = [jnp.where(lane_head == a, state, 0.0) for a in range(BLOCK // HEAD_DIM)]
                blocks.append(jnp.concatenate(heads, axis=0).astype(BF16))
            if len(blocks) == 2:
                blocks = [jnp.concatenate([blocks[0], zeros], axis=1), jnp.concatenate([zeros, blocks[1]], axis=1)]
            linear = jnp.dot(q_v[:, at : at + size], jnp.concatenate(blocks, axis=0), preferred_element_type=F32)
            squares = linear * linear
            squares = squares[:, :BLOCK] + squares[:, BLOCK:] if size == CHUNK else squares
            ssq_v[...] = squares if at == 0 else ssq_v[...] + squares
            gain = out_gain[at : at + size].astype(F32)
            lin_v[:, at : at + size] = (linear * gain).astype(BF16)

    def mix(g):
        first, last = GROUPS[g]
        rows_of = slice(first * BLOCK, last * BLOCK)
        for at, size in chunks_of(0, width):
            done = jnp.dot(lin_v[:, rows_of], wo_v[rows_of, at : at + size], preferred_element_type=F32)
            acc_v[:, at : at + size] = done if g == 0 else acc_v[:, at : at + size] + done

    def finish(g):
        first, last = GROUPS[g]
        rows_of = slice(first * BLOCK, last * BLOCK)
        ssq = jnp.sum(ssq_v[...], axis=1, keepdims=True) / width
        factor2 = r2_v[...]
        r2_v[...] = jnp.sqrt(factor2) * lax.rsqrt(factor2 * ssq + EPSILON)
        for at, size in chunks_of(0, width):
            done = jnp.dot(lin_v[:, rows_of], wo_v[rows_of, at : at + size], preferred_element_type=F32)
            for col in range(0, size, BLOCK):
                here = slice(at + col, at + col + BLOCK)
                piece = (acc_v[:, here] + done[:, col : col + BLOCK]) * r2_v[...]
                out_v[0, :, here] = (x_v[:, here].astype(F32) + piece).astype(BF16)

    x_copy.wait()
    for copy in w_copies[0]:
        copy.wait()
    total = jnp.zeros((rows, BLOCK), F32)
    for col in range(0, width, BLOCK):
        piece = x_v[:, col : col + BLOCK].astype(F32)
        total += piece * piece
        xg_v[:, col : col + BLOCK] = (piece * norm_gain[col : col + BLOCK].astype(F32)).astype(BF16)
    mean = jnp.sum(total, axis=1, keepdims=True) / width
    r2_v[...] = jnp.broadcast_to(1.0 / (mean + EPSILON), (rows, BLOCK))
    wq_copy.start()
    wo_copy.start()
    project(0)
    for copy in w_copies[1]:
        copy.wait()
    if comm:
        pl.semaphore_wait(barrier, 2 * (PEERS - 1))
    send_parts(0)
    project(1)
    send_parts(1)
    wq_copy.wait()
    for at, size in chunks_of(0, width):
        done = jnp.dot(xg_v[...], wq_v[:, at : at + size], preferred_element_type=F32)
        q_v[:, at : at + size] = jnp.maximum(done, 0.0).astype(BF16)
    wo_copy.wait()
    if comm:
        each_group(send_share)
        each_group(send_causal)
        each_group(sent)
        whole_copies(0).wait_recv()
    attend(0)
    mix(0)
    if comm:
        whole_copies(1).wait_recv()
    attend(1)
    finish(1)


def make_call(rows, width, comm=True):
    n_groups = len(GROUPS)
    vm = pltpu.VMEM
    dma = pltpu.SemaphoreType.DMA
    slots = vm((n_groups, PEERS * DEEP, BLOCK), F32)
    scratch = [
        vm((rows, width), BF16),
        vm((rows, width), BF16),
        vm((width, 2 * width), BF16),
        vm((width, width), BF16),
        vm((width, width), BF16),
        vm((rows, 2 * width), BF16),
        vm((rows, width), BF16),
        vm((rows, width), BF16),
        vm((rows, width), F32),
        vm((rows, BLOCK), F32),
        vm((rows, BLOCK), F32),
        slots, slots, vm((n_groups, DEEP, BLOCK), F32), slots, slots,
        dma, dma((n_groups, 2)), dma, dma,
        dma((n_groups,)), dma((n_groups,)), dma((n_groups, PEERS)), dma((n_groups, PEERS)), dma((n_groups,)), dma((n_groups,)),
    ]
    hbm = pl.BlockSpec(memory_space=pltpu.HBM)
    vec = pl.BlockSpec(memory_space=pltpu.VMEM)
    return pl.pallas_call(
        functools.partial(kernel, comm),
        out_shape=pltpu.VMEM((1, rows, width), BF16),
        in_specs=[hbm, vec, hbm, vec, hbm],
        out_specs=vec,
        scratch_shapes=scratch,
        compiler_params=pltpu.CompilerParams(
            collective_id=0 if comm else None, has_side_effects=comm, vmem_limit_bytes=48 * 2**20
        ),
        cost_estimate=pl.CostEstimate(flops=10**10, bytes_accessed=15 * 10**6, transcendentals=0),
    )


def body(frames_in, norm_gain, w_qkv, out_gain, w_out):
    call = make_call(frames_in.shape[1], frames_in.shape[2])
    return call(frames_in, norm_gain, w_qkv, out_gain, w_out)


def solution(mesh):
    in_specs = (P("tm", "rows", None), P(), P(), P(), P())
    out_specs = P("tm", "rows", None)
    return jax.shard_map(body, mesh=mesh, in_specs=in_specs, out_specs=out_specs, check_vma=False)
```

```python
import functools

import jax
import jax.numpy as jnp
from jax import lax
from jax.experimental import pallas as pl
from jax.experimental.pallas import tpu as pltpu
from jax.sharding import PartitionSpec as P

HEAD_DIM = 32
EPSILON = 1e-06
BLOCK = 128
COUNT = 3
DEEP = 8
PEERS = 16
SIDE = 4
F32, BF16 = jnp.float32, jnp.bfloat16
MESH = pl.DeviceIdType.MESH
AWAY = sorted(
    ((dx, dy) for dx in range(SIDE) for dy in range(SIDE) if dx or dy),
    key=lambda d: -sum(min(a, SIDE - a) for a in d),
)


def kernel(
    comm,
    x_hbm, norm_gain_hbm, wqkv_hbm, out_gain_hbm, wout_hbm, out_v,
    x_v, xg_v, w_v, wq_v, wo_v, kv_v, q_v, lin_v, acc_v, r2_v, ssq_v, norm_gain, out_gain, gain_v,
    sends, parts, owns, shares, wholes,
    x_sem, gain_sem, w_sem, wq_sem, wo_sem, s1, r1, s2, r2, s3, r3,
):
    rows, width = x_v.shape
    n_groups, _, wide = q_v.shape
    frame, band = (lax.axis_index("tm"), lax.axis_index("rows")) if comm else (0, 0)

    gain_copies = [
        pltpu.make_async_copy(norm_gain_hbm, norm_gain, gain_sem.at[0]),
        pltpu.make_async_copy(out_gain_hbm, out_gain, gain_sem.at[1]),
    ]
    x_copy = pltpu.make_async_copy(x_hbm.at[0], x_v, x_sem)
    for copy in gain_copies:
        copy.start()
    x_copy.start()

    def w_copy(g, part):
        src = wqkv_hbm.at[:, pl.ds(pl.multiple_of((2 - part) * width + g * wide, BLOCK), wide)]
        dst = w_v.at[g, :, pl.ds(part * wide, wide)] if part < 2 else wq_v.at[g]
        return pltpu.make_async_copy(src, dst, w_sem.at[g, part] if part < 2 else wq_sem.at[g])

    def wo_copy(g):
        src = wout_hbm.at[pl.ds(pl.multiple_of(g * wide, BLOCK), wide)]
        return pltpu.make_async_copy(src, wo_v.at[g], wo_sem.at[g])

    for g in range(n_groups):
        for part in range(2):
            w_copy(g, part).start()

    if comm:
        barrier = pltpu.get_barrier_semaphore()

        def greet(k, _):
            pl.semaphore_signal(barrier, inc=1, device_id={"rows": lax.rem(band + k, PEERS)}, device_id_type=MESH)
            pl.semaphore_signal(barrier, inc=1, device_id={"tm": lax.rem(frame + k, PEERS)}, device_id_type=MESH)
            return _

        lax.fori_loop(1, PEERS, greet, 0)

    others = [lax.rem(band // SIDE + dx, SIDE) * SIDE + lax.rem(band + dy, SIDE) for dx, dy in AWAY]

    def mesh_copy(src, dst, send_sem, recv_sem, where):
        return pltpu.make_async_remote_copy(
            src_ref=src, dst_ref=dst, send_sem=send_sem, recv_sem=recv_sem, device_id=where, device_id_type=MESH
        )

    def slot(buf, g, index):
        return buf.at[g, pl.ds(pl.multiple_of(index * DEEP, 8), DEEP)]

    def bulk(buf, g):
        return buf.at[g, pl.ds(0, (PEERS - 1) * DEEP)]

    def part_copies(g):
        return mesh_copy(bulk(sends, g), bulk(parts, g), s1.at[g], r1.at[g], {"rows": band})

    def share_copy(g, source, to):
        return mesh_copy(owns.at[g], slot(shares, g, source), s2.at[g, to], r2.at[g, source], {"tm": to})

    def whole_copies(g):
        return mesh_copy(bulk(wholes, g), bulk(wholes, g), s3.at[g], r3.at[g], {"rows": band})

    def send_parts(g):
        for k, to in enumerate(others):
            mesh_copy(slot(sends, g, to), slot(parts, g, k), s1.at[g], r1.at[g], {"rows": to}).start()

    def send_share(g):
        part_copies(g).wait_recv()
        total = slot(sends, g, band)[...]
        for k in range(PEERS - 1):
            total += slot(parts, g, k)[...]
        owns[g] = total

        def send(to, _):
            share_copy(g, frame, to).start()
            return _

        lax.fori_loop(frame + 1, PEERS, send, 0)

    def send_causal(g):
        def arrived(i, _):
            share_copy(g, i, i).wait_recv()
            return _

        lax.fori_loop(0, frame, arrived, 0)
        total = owns[g]
        for i in range(PEERS - 1):
            total += jnp.where(i < frame, slot(shares, g, i)[...], 0.0)
        mine = slot(wholes, g, band)
        mine[...] = total
        for to in others:
            mesh_copy(mine, mine, s3.at[g], r3.at[g], {"rows": to}).start()

    def sent(g):
        part_copies(g).wait_send()

        def gone(to, _):
            share_copy(g, frame, to).wait_send()
            return _

        lax.fori_loop(frame + 1, PEERS, gone, 0)
        whole_copies(g).wait_send()

    def each_group(step):
        def one(g, _):
            step(g)
            return _

        lax.fori_loop(0, n_groups, one, 0)

    lane_head = lax.broadcasted_iota(jnp.int32, (HEAD_DIM, BLOCK), 1) // HEAD_DIM

    def project(g):
        for part in range(2):
            w_copy(g, part).wait()
        done = jnp.dot(xg_v[...], w_v[g], preferred_element_type=F32)
        for col in range(0, 2 * wide, BLOCK):
            piece = done[:, col : col + BLOCK]
            if col >= wide:
                piece = jnp.maximum(piece, 0.0) * r2_v[...]
            kv_v[:, col : col + BLOCK] = piece.astype(BF16)
        for j in range(COUNT):
            block = lax.dot_general(
                kv_v[:, wide + j * BLOCK : wide + (j + 1) * BLOCK], kv_v[:, j * BLOCK : (j + 1) * BLOCK],
                (((0,), (0,)), ((), ())), preferred_element_type=F32,
            )
            state = jnp.where(lane_head == 0, block[:HEAD_DIM], 0.0)
            for a in range(1, BLOCK // HEAD_DIM):
                state += jnp.where(lane_head == a, block[a * HEAD_DIM : (a + 1) * HEAD_DIM], 0.0)
            for half in range(2):
                sends[g, pl.ds(2 * j + half, PEERS, stride=DEEP), :] = state[half * PEERS : (half + 1) * PEERS]
        if comm:

            @pl.when(g == 1)
            def _():
                pl.semaphore_wait(barrier, 2 * (PEERS - 1))
                send_parts(0)

            @pl.when(g >= 1)
            def _():
                send_parts(g)

    def query(g):
        w_copy(g, 2).wait()
        done = jnp.dot(xg_v[...], wq_v[g], preferred_element_type=F32)
        q_v[g] = jnp.maximum(done, 0.0).astype(BF16)
        if comm:
            send_share(g)

    def attend(g):
        wo_copy(g).wait()
        if comm:
            whole_copies(g).wait_recv()
        whole = wholes if comm else sends
        blocks = []
        for j in range(COUNT):
            state = jnp.concatenate([whole[g, pl.ds(2 * j + half, PEERS, stride=DEEP), :] for half in range(2)], axis=0)
            heads = [jnp.where(lane_head == a, state, 0.0) for a in range(BLOCK // HEAD_DIM)]
            blocks.append(jnp.concatenate(heads, axis=0).astype(BF16))
        zeros = jnp.zeros((BLOCK, BLOCK), BF16)
        squares = ssq_v[...]
        for j in range(0, COUNT, 2):
            here = slice(j * BLOCK, min(j + 2, COUNT) * BLOCK)
            states = blocks[j]
            if j + 1 < COUNT:
                upper = jnp.concatenate([states, zeros], axis=1)
                states = jnp.concatenate([upper, jnp.concatenate([zeros, blocks[j + 1]], axis=1)], axis=0)
            linear = jnp.dot(q_v[g, :, here], states, preferred_element_type=F32)
            for col in range(0, linear.shape[1], BLOCK):
                piece = linear[:, col : col + BLOCK]
                squares += piece * piece
            lin_v[:, here] = (linear * gain_v[g, :, here]).astype(BF16)
        ssq_v[...] = squares
        factor2 = r2_v[...]
        mean = jnp.sum(squares, axis=1, keepdims=True) / width
        scale = jnp.sqrt(factor2) * lax.rsqrt(factor2 * mean + EPSILON)
        for col in range(0, width, 2 * BLOCK):
            here = slice(col, min(col + 2 * BLOCK, width))
            done = jnp.dot(lin_v[...], wo_v[g, :, here], preferred_element_type=F32)
            total = acc_v[:, here] + done
            acc_v[:, here] = total
            for at in range(col, here.stop, BLOCK):
                piece = x_v[:, at : at + BLOCK].astype(F32) + total[:, at - col : at - col + BLOCK] * scale
                out_v[0, :, at : at + BLOCK] = piece.astype(BF16)

    for copy in gain_copies:
        copy.wait()
    x_copy.wait()
    total = jnp.zeros((rows, BLOCK), F32)
    for col in range(0, width, BLOCK):
        piece = x_v[:, col : col + BLOCK].astype(F32)
        total += piece * piece
        xg_v[:, col : col + BLOCK] = (piece * norm_gain[col : col + BLOCK].astype(F32)).astype(BF16)
    mean = jnp.sum(total, axis=1, keepdims=True) / width
    r2_v[...] = jnp.broadcast_to(1.0 / (mean + EPSILON), (rows, BLOCK))
    for g in range(n_groups):
        w_copy(g, 2).start()
    for g in range(n_groups):
        wo_copy(g).start()
        gain_v[g, 0] = out_gain[g * wide : (g + 1) * wide].astype(F32)
    ssq_v[...] = jnp.zeros_like(ssq_v)
    each_group(project)
    each_group(query)
    if comm:
        each_group(send_causal)
    acc_v[...] = jnp.zeros_like(acc_v)
    if comm:
        each_group(sent)
    each_group(attend)


def make_call(rows, width, comm=True):
    wide = COUNT * BLOCK
    n_groups = width // wide
    vm = pltpu.VMEM
    dma = pltpu.SemaphoreType.DMA
    each = dma((n_groups,))
    slots = vm((n_groups, PEERS * DEEP, BLOCK), F32)
    scratch = [
        vm((rows, width), BF16),
        vm((rows, width), BF16),
        vm((n_groups, width, 2 * wide), BF16),
        vm((n_groups, width, wide), BF16),
        vm((n_groups, wide, width), BF16),
        vm((rows, 2 * wide), BF16),
        vm((n_groups, rows, wide), BF16),
        vm((rows, wide), BF16),
        vm((rows, width), F32),
        vm((rows, BLOCK), F32),
        vm((rows, BLOCK), F32),
        vm((width,), BF16), vm((width,), BF16), vm((n_groups, 1, wide), F32),
        slots, slots, vm((n_groups, DEEP, BLOCK), F32), slots, slots,
        dma, dma((2,)), dma((n_groups, 2)), each, each,
        each, each, dma((n_groups, PEERS)), dma((n_groups, PEERS)), each, each,
    ]
    hbm = pl.BlockSpec(memory_space=pltpu.HBM)
    return pl.pallas_call(
        functools.partial(kernel, comm),
        out_shape=pltpu.VMEM((1, rows, width), BF16),
        in_specs=[hbm] * 5,
        out_specs=pl.BlockSpec(memory_space=pltpu.VMEM),
        scratch_shapes=scratch,
        compiler_params=pltpu.CompilerParams(
            collective_id=0 if comm else None, has_side_effects=comm, vmem_limit_bytes=60 * 2**20
        ),
        cost_estimate=pl.CostEstimate(flops=10**10, bytes_accessed=15 * 10**6, transcendentals=0),
    )


def body(frames_in, norm_gain, w_qkv, out_gain, w_out):
    call = make_call(frames_in.shape[1], frames_in.shape[2])
    return call(frames_in, norm_gain, w_qkv, out_gain, w_out)


def solution(mesh):
    in_specs = (P("tm", "rows", None), P(), P(), P(), P())
    out_specs = P("tm", "rows", None)
    return jax.shard_map(body, mesh=mesh, in_specs=in_specs, out_specs=out_specs, check_vma=False)
```

```python
import functools

import jax
import jax.numpy as jnp
from jax import lax
from jax.experimental import pallas as pl
from jax.experimental.pallas import tpu as pltpu
from jax.sharding import PartitionSpec as P

HEAD_DIM = 32
EPSILON = 1e-06
BLOCK = 128
COUNT = 3
DEEP = 8
PEERS = 16
SIDE = 4
F32, BF16 = jnp.float32, jnp.bfloat16
MESH = pl.DeviceIdType.MESH
AWAY = sorted(
    ((dx, dy) for dx in range(SIDE) for dy in range(SIDE) if dx or dy),
    key=lambda d: -sum(min(a, SIDE - a) for a in d),
)


def kernel(
    comm,
    x_hbm, norm_gain_hbm, wqkv_hbm, out_gain_hbm, wout_hbm, out_v,
    x_v, xg_v, kt_v, w_v, wq_v, wo_v, kv_v, q_v, lin_v, acc_v, r2_v, ssq_v, norm_gain, out_gain, gain_v,
    sends, parts, owns, shares, wholes,
    x_sem, gain_sem, w_sem, wq_sem, wo_sem, s1, r1, s2, r2, s3, r3,
):
    rows, width = x_v.shape
    n_groups, _, wide = q_v.shape
    frame, band = (lax.axis_index("tm"), lax.axis_index("rows")) if comm else (0, 0)

    gain_copies = [
        pltpu.make_async_copy(norm_gain_hbm, norm_gain, gain_sem.at[0]),
        pltpu.make_async_copy(out_gain_hbm, out_gain, gain_sem.at[1]),
    ]
    x_copy = pltpu.make_async_copy(x_hbm.at[0], x_v, x_sem)
    for copy in gain_copies:
        copy.start()
    x_copy.start()

    def w_copy(g, part):
        src = wqkv_hbm.at[:, pl.ds(pl.multiple_of((1, 2, 0)[part] * width + g * wide, BLOCK), wide)]
        dst = w_v.at[g, :, pl.ds(part * wide, wide)] if part < 2 else wq_v.at[g]
        return pltpu.make_async_copy(src, dst, w_sem.at[g, part] if part < 2 else wq_sem.at[g])

    def wo_copy(g):
        src = wout_hbm.at[pl.ds(pl.multiple_of(g * wide, BLOCK), wide)]
        return pltpu.make_async_copy(src, wo_v.at[g], wo_sem.at[g])

    for part in range(2):
        w_copy(0, part).start()

    if comm:
        barrier = pltpu.get_barrier_semaphore()

        def greet(k, _):
            pl.semaphore_signal(barrier, inc=1, device_id={"rows": lax.rem(band + k, PEERS)}, device_id_type=MESH)
            pl.semaphore_signal(barrier, inc=1, device_id={"tm": lax.rem(frame + k, PEERS)}, device_id_type=MESH)
            return _

        lax.fori_loop(1, PEERS, greet, 0)

    others = [lax.rem(band // SIDE + dx, SIDE) * SIDE + lax.rem(band + dy, SIDE) for dx, dy in AWAY]

    def mesh_copy(src, dst, send_sem, recv_sem, where):
        return pltpu.make_async_remote_copy(
            src_ref=src, dst_ref=dst, send_sem=send_sem, recv_sem=recv_sem, device_id=where, device_id_type=MESH
        )

    def slot(buf, g, index):
        return buf.at[g, pl.ds(pl.multiple_of(index * DEEP, 8), DEEP)]

    def bulk(buf, g):
        return buf.at[g, pl.ds(0, (PEERS - 1) * DEEP)]

    def part_copies(g):
        return mesh_copy(bulk(sends, g), bulk(parts, g), s1.at[g], r1.at[g], {"rows": band})

    def share_copy(g, source, to):
        return mesh_copy(owns.at[g], slot(shares, g, source), s2.at[g, to], r2.at[g, source], {"tm": to})

    def whole_copies(g):
        return mesh_copy(bulk(wholes, g), bulk(wholes, g), s3.at[g], r3.at[g], {"rows": band})

    def send_parts(g):
        for k, to in enumerate(others):
            mesh_copy(slot(sends, g, to), slot(parts, g, k), s1.at[g], r1.at[g], {"rows": to}).start()

    def send_share(g):
        part_copies(g).wait_recv()
        total = slot(sends, g, band)[...]
        for k in range(PEERS - 1):
            total += slot(parts, g, k)[...]
        owns[g] = total

        def send(to, _):
            share_copy(g, frame, to).start()
            return _

        lax.fori_loop(frame + 1, PEERS, send, 0)

    def send_causal(g):
        def arrived(i, _):
            share_copy(g, i, i).wait_recv()
            return _

        lax.fori_loop(0, frame, arrived, 0)
        total = owns[g]
        for i in range(PEERS - 1):
            total += jnp.where(i < frame, slot(shares, g, i)[...], 0.0)
        mine = slot(wholes, g, band)
        mine[...] = total
        for to in others:
            mesh_copy(mine, mine, s3.at[g], r3.at[g], {"rows": to}).start()

    def sent(g):
        part_copies(g).wait_send()

        def gone(to, _):
            share_copy(g, frame, to).wait_send()
            return _

        lax.fori_loop(frame + 1, PEERS, gone, 0)
        whole_copies(g).wait_send()

    def each_group(step):
        def one(g, _):
            step(g)
            return _

        lax.fori_loop(0, n_groups, one, 0)

    lane_head = lax.broadcasted_iota(jnp.int32, (HEAD_DIM, BLOCK), 1) // HEAD_DIM

    def project(g):
        for part in range(2):
            w_copy(g, part).wait()

        @pl.when(g == 0)
        def _():
            for part in range(2):
                w_copy(2, part).start()

        @pl.when(g == 1)
        def _():
            for i in range(n_groups):
                w_copy(i, 2).start()

        @pl.when(g == 2)
        def _():
            for i in range(n_groups):
                wo_copy(i).start()

        for at in range(0, 2 * wide, 2 * BLOCK):
            for top in range(0, rows, 416):
                done = jnp.dot(xg_v[top : top + 416], w_v[g, :, at : at + 2 * BLOCK], preferred_element_type=F32)
                for col in range(at, at + 2 * BLOCK, BLOCK):
                    piece = done[:, col - at : col - at + BLOCK]
                    if col < wide:
                        kv_v[top : top + 416, col : col + BLOCK] = (jnp.maximum(piece, 0.0) * r2_v[top : top + 416]).astype(BF16)
                    else:
                        kv_v[top : top + 416, col : col + BLOCK] = piece.astype(BF16)
            if at + 2 * BLOCK <= wide + BLOCK:
                for j in range(at // BLOCK, min(at // BLOCK + 2, COUNT)):
                    kt_v[j] = kv_v[:, j * BLOCK : (j + 1) * BLOCK].T
        for j in range(COUNT):
            block = jnp.dot(kt_v[j], kv_v[:, wide + j * BLOCK : wide + (j + 1) * BLOCK], preferred_element_type=F32)
            state = jnp.where(lane_head == 0, block[:HEAD_DIM], 0.0)
            for a in range(1, BLOCK // HEAD_DIM):
                state += jnp.where(lane_head == a, block[a * HEAD_DIM : (a + 1) * HEAD_DIM], 0.0)
            for half in range(2):
                sends[g, pl.ds(2 * j + half, PEERS, stride=DEEP), :] = state[half * PEERS : (half + 1) * PEERS]
        if comm:

            @pl.when(g == 1)
            def _():
                pl.semaphore_wait(barrier, 2 * (PEERS - 1))
                send_parts(0)

            @pl.when(g >= 1)
            def _():
                send_parts(g)

    def query(g):
        w_copy(g, 2).wait()
        done = jnp.dot(xg_v[...], wq_v[g], preferred_element_type=F32)
        q_v[g] = jnp.maximum(done, 0.0).astype(BF16)
        if comm:
            send_share(g)

    def attend(g):
        wo_copy(g).wait()
        if comm:
            whole_copies(g).wait_recv()
        whole = wholes if comm else sends
        blocks = []
        for j in range(COUNT):
            state = jnp.concatenate([whole[g, pl.ds(2 * j + half, PEERS, stride=DEEP), :] for half in range(2)], axis=0)
            heads = [jnp.where(lane_head == a, state, 0.0) for a in range(BLOCK // HEAD_DIM)]
            blocks.append(jnp.concatenate(heads, axis=0).astype(BF16))
        zeros = jnp.zeros((BLOCK, BLOCK), BF16)
        squares = ssq_v[...]
        for j in range(0, COUNT, 2):
            here = slice(j * BLOCK, min(j + 2, COUNT) * BLOCK)
            states = blocks[j]
            if j + 1 < COUNT:
                upper = jnp.concatenate([states, zeros], axis=1)
                states = jnp.concatenate([upper, jnp.concatenate([zeros, blocks[j + 1]], axis=1)], axis=0)
            linear = jnp.dot(q_v[g, :, here], states, preferred_element_type=F32)
            for col in range(0, linear.shape[1], BLOCK):
                piece = linear[:, col : col + BLOCK]
                squares += piece * piece
            lin_v[:, here] = (linear * gain_v[g, :, here]).astype(BF16)
        ssq_v[...] = squares
        factor2 = r2_v[...]
        mean = jnp.sum(squares, axis=1, keepdims=True) / width
        scale = jnp.sqrt(factor2) * lax.rsqrt(factor2 * mean + EPSILON)
        for col in range(0, width, 2 * BLOCK):
            here = slice(col, min(col + 2 * BLOCK, width))
            done = jnp.dot(lin_v[...], wo_v[g, :, here], preferred_element_type=F32)
            total = acc_v[:, here] + done
            acc_v[:, here] = total
            for at in range(col, here.stop, BLOCK):
                piece = x_v[:, at : at + BLOCK].astype(F32) + total[:, at - col : at - col + BLOCK] * scale
                out_v[0, :, at : at + BLOCK] = piece.astype(BF16)

    for copy in gain_copies:
        copy.wait()
    x_copy.wait()
    for part in range(2):
        w_copy(1, part).start()
    total = jnp.zeros((rows, BLOCK), F32)
    for col in range(0, width, BLOCK):
        piece = x_v[:, col : col + BLOCK].astype(F32)
        total += piece * piece
        xg_v[:, col : col + BLOCK] = (piece * norm_gain[col : col + BLOCK].astype(F32)).astype(BF16)
    mean = jnp.sum(total, axis=1, keepdims=True) / width
    r2_v[...] = jnp.broadcast_to(1.0 / (mean + EPSILON), (rows, BLOCK))
    for g in range(n_groups):
        gain_v[g, 0] = out_gain[g * wide : (g + 1) * wide].astype(F32)
    ssq_v[...] = jnp.zeros_like(ssq_v)
    each_group(project)
    each_group(query)
    if comm:
        each_group(send_causal)
    acc_v[...] = jnp.zeros_like(acc_v)
    if comm:
        each_group(sent)
    each_group(attend)


def make_call(rows, width, comm=True):
    wide = COUNT * BLOCK
    n_groups = width // wide
    vm = pltpu.VMEM
    dma = pltpu.SemaphoreType.DMA
    each = dma((n_groups,))
    slots = vm((n_groups, PEERS * DEEP, BLOCK), F32)
    scratch = [
        vm((rows, width), BF16),
        vm((rows, width), BF16),
        vm((COUNT, BLOCK, rows), BF16),
        vm((n_groups, width, 2 * wide), BF16),
        vm((n_groups, width, wide), BF16),
        vm((n_groups, wide, width), BF16),
        vm((rows, 2 * wide), BF16),
        vm((n_groups, rows, wide), BF16),
        vm((rows, wide), BF16),
        vm((rows, width), F32),
        vm((rows, BLOCK), F32),
        vm((rows, BLOCK), F32),
        vm((width,), BF16), vm((width,), BF16), vm((n_groups, 1, wide), F32),
        slots, slots, vm((n_groups, DEEP, BLOCK), F32), slots, slots,
        dma, dma((2,)), dma((n_groups, 2)), each, each,
        each, each, dma((n_groups, PEERS)), dma((n_groups, PEERS)), each, each,
    ]
    hbm = pl.BlockSpec(memory_space=pltpu.HBM)
    return pl.pallas_call(
        functools.partial(kernel, comm),
        out_shape=pltpu.VMEM((1, rows, width), BF16),
        in_specs=[hbm] * 5,
        out_specs=pl.BlockSpec(memory_space=pltpu.VMEM),
        scratch_shapes=scratch,
        compiler_params=pltpu.CompilerParams(
            collective_id=0 if comm else None, has_side_effects=comm, vmem_limit_bytes=60 * 2**20
        ),
        cost_estimate=pl.CostEstimate(flops=10**10, bytes_accessed=15 * 10**6, transcendentals=0),
    )


def body(frames_in, norm_gain, w_qkv, out_gain, w_out):
    call = make_call(frames_in.shape[1], frames_in.shape[2])
    return call(frames_in, norm_gain, w_qkv, out_gain, w_out)


def solution(mesh):
    in_specs = (P("tm", "rows", None), P(), P(), P(), P())
    out_specs = P("tm", "rows", None)
    return jax.shard_map(body, mesh=mesh, in_specs=in_specs, out_specs=out_specs, check_vma=False)
```

```python
import functools

import jax
import jax.numpy as jnp
from jax import lax
from jax.experimental import pallas as pl
from jax.experimental.pallas import tpu as pltpu
from jax.sharding import PartitionSpec as P

HEAD_DIM = 32
EPSILON = 1e-06
BLOCK = 128
COUNT = 3
DEEP = 8
PEERS = 16
SIDE = 4
F32, BF16 = jnp.float32, jnp.bfloat16
MESH = pl.DeviceIdType.MESH
AWAY = sorted(
    ((dx, dy) for dx in range(SIDE) for dy in range(SIDE) if dx or dy),
    key=lambda d: -sum(min(a, SIDE - a) for a in d),
)


def kernel(
    comm,
    x_hbm, norm_gain_hbm, wqkv_hbm, out_gain_hbm, wout_hbm, out_v,
    x_v, xg_v, kt_v, w_v, wq_v, wo_v, kv_v, q_v, lin_v, acc_v, r2_v, ssq_v, norm_gain, out_gain, gain_v,
    sends, parts, owns, shares, wholes,
    x_sem, gain_sem, w_sem, wq_sem, wo_sem, s1, r1, s2, r2, s3, r3,
):
    rows, width = x_v.shape
    n_groups, _, wide = q_v.shape
    frame, band = (lax.axis_index("tm"), lax.axis_index("rows")) if comm else (0, 0)

    gain_copies = [
        pltpu.make_async_copy(norm_gain_hbm, norm_gain, gain_sem.at[0]),
        pltpu.make_async_copy(out_gain_hbm, out_gain, gain_sem.at[1]),
    ]
    x_copy = pltpu.make_async_copy(x_hbm.at[0], x_v, x_sem)
    for copy in gain_copies:
        copy.start()
    x_copy.start()

    def w_copy(g, part):
        src = wqkv_hbm.at[:, pl.ds(pl.multiple_of((1 + part) * width + g * wide, BLOCK), wide)]
        return pltpu.make_async_copy(src, w_v.at[g, :, pl.ds(part * wide, wide)], w_sem.at[g, part])

    wq_copy = pltpu.make_async_copy(wqkv_hbm.at[:, pl.ds(0, width)], wq_v, wq_sem)

    def wo_copy(g):
        src = wout_hbm.at[pl.ds(pl.multiple_of(g * wide, BLOCK), wide)]
        return pltpu.make_async_copy(src, wo_v.at[g], wo_sem.at[g])

    for part in range(2):
        w_copy(0, part).start()

    if comm:
        barrier = pltpu.get_barrier_semaphore()

        def greet(k, _):
            pl.semaphore_signal(barrier, inc=1, device_id={"rows": lax.rem(band + k, PEERS)}, device_id_type=MESH)
            pl.semaphore_signal(barrier, inc=1, device_id={"tm": lax.rem(frame + k, PEERS)}, device_id_type=MESH)
            return _

        lax.fori_loop(1, PEERS, greet, 0)

    others = [lax.rem(band // SIDE + dx, SIDE) * SIDE + lax.rem(band + dy, SIDE) for dx, dy in AWAY]

    def mesh_copy(src, dst, send_sem, recv_sem, where):
        return pltpu.make_async_remote_copy(
            src_ref=src, dst_ref=dst, send_sem=send_sem, recv_sem=recv_sem, device_id=where, device_id_type=MESH
        )

    def slot(buf, g, index):
        return buf.at[g, pl.ds(pl.multiple_of(index * DEEP, 8), DEEP)]

    def bulk(buf, g):
        return buf.at[g, pl.ds(0, (PEERS - 1) * DEEP)]

    def part_copies(g):
        return mesh_copy(bulk(sends, g), bulk(parts, g), s1.at[g], r1.at[g], {"rows": band})

    def share_copy(g, source, to):
        return mesh_copy(owns.at[g], slot(shares, g, source), s2.at[g, to], r2.at[g, source], {"tm": to})

    def whole_copies(g):
        return mesh_copy(bulk(wholes, g), bulk(wholes, g), s3.at[g], r3.at[g], {"rows": band})

    def send_parts(g):
        for k, to in enumerate(others):
            mesh_copy(slot(sends, g, to), slot(parts, g, k), s1.at[g], r1.at[g], {"rows": to}).start()

    def send_share(g):
        part_copies(g).wait_recv()
        total = slot(sends, g, band)[...]
        for k in range(PEERS - 1):
            total += slot(parts, g, k)[...]
        owns[g] = total

        def send(to, _):
            share_copy(g, frame, to).start()
            return _

        lax.fori_loop(frame + 1, PEERS, send, 0)

    def send_causal(g):
        def arrived(i, _):
            share_copy(g, i, i).wait_recv()
            return _

        lax.fori_loop(0, frame, arrived, 0)
        total = owns[g]
        for i in range(PEERS - 1):
            total += jnp.where(i < frame, slot(shares, g, i)[...], 0.0)
        mine = slot(wholes, g, band)
        mine[...] = total
        for to in others:
            mesh_copy(mine, mine, s3.at[g], r3.at[g], {"rows": to}).start()

    def sent(g):
        part_copies(g).wait_send()

        def gone(to, _):
            share_copy(g, frame, to).wait_send()
            return _

        lax.fori_loop(frame + 1, PEERS, gone, 0)
        whole_copies(g).wait_send()

    def each_group(step):
        def one(g, _):
            step(g)
            return _

        lax.fori_loop(0, n_groups, one, 0)

    lane_head = lax.broadcasted_iota(jnp.int32, (HEAD_DIM, BLOCK), 1) // HEAD_DIM

    def project(g):
        for part in range(2):
            w_copy(g, part).wait()

        @pl.when(g == 0)
        def _():
            for part in range(2):
                w_copy(2, part).start()

        @pl.when(g == 1)
        def _():
            wq_copy.start()

        @pl.when(g == 2)
        def _():
            for i in range(n_groups):
                wo_copy(i).start()

        for at in range(0, 2 * wide, 2 * BLOCK):
            for top in range(0, rows, 416):
                done = jnp.dot(xg_v[top : top + 416], w_v[g, :, at : at + 2 * BLOCK], preferred_element_type=F32)
                for col in range(at, at + 2 * BLOCK, BLOCK):
                    piece = done[:, col - at : col - at + BLOCK]
                    if col < wide:
                        kv_v[top : top + 416, col : col + BLOCK] = (jnp.maximum(piece, 0.0) * r2_v[top : top + 416]).astype(BF16)
                    else:
                        kv_v[top : top + 416, col : col + BLOCK] = piece.astype(BF16)
            if at + 2 * BLOCK <= wide + BLOCK:
                for j in range(at // BLOCK, min(at // BLOCK + 2, COUNT)):
                    kt_v[j] = kv_v[:, j * BLOCK : (j + 1) * BLOCK].T
        for j in range(COUNT):
            block = jnp.dot(kt_v[j], kv_v[:, wide + j * BLOCK : wide + (j + 1) * BLOCK], preferred_element_type=F32)
            state = jnp.where(lane_head == 0, block[:HEAD_DIM], 0.0)
            for a in range(1, BLOCK // HEAD_DIM):
                state += jnp.where(lane_head == a, block[a * HEAD_DIM : (a + 1) * HEAD_DIM], 0.0)
            for half in range(2):
                sends[g, pl.ds(2 * j + half, PEERS, stride=DEEP), :] = state[half * PEERS : (half + 1) * PEERS]
        if comm:

            @pl.when(g == 1)
            def _():
                pl.semaphore_wait(barrier, 2 * (PEERS - 1))
                send_parts(0)

            @pl.when(g >= 1)
            def _():
                send_parts(g)

    def query():
        wq_copy.wait()
        for at in range(0, width, 2 * BLOCK):
            stop = min(at + 2 * BLOCK, width)
            done = jnp.dot(xg_v[...], wq_v[:, at:stop], preferred_element_type=F32)
            for col in range(at, stop, BLOCK):
                piece = jnp.maximum(done[:, col - at : col - at + BLOCK], 0.0).astype(BF16)
                q_v[col // wide, :, col % wide : col % wide + BLOCK] = piece

    def attend(g):
        wo_copy(g).wait()
        if comm:
            whole_copies(g).wait_recv()
        whole = wholes if comm else sends
        blocks = []
        for j in range(COUNT):
            state = jnp.concatenate([whole[g, pl.ds(2 * j + half, PEERS, stride=DEEP), :] for half in range(2)], axis=0)
            heads = [jnp.where(lane_head == a, state, 0.0) for a in range(BLOCK // HEAD_DIM)]
            blocks.append(jnp.concatenate(heads, axis=0).astype(BF16))
        zeros = jnp.zeros((BLOCK, BLOCK), BF16)
        squares = ssq_v[...]
        for j in range(0, COUNT, 2):
            here = slice(j * BLOCK, min(j + 2, COUNT) * BLOCK)
            states = blocks[j]
            if j + 1 < COUNT:
                upper = jnp.concatenate([states, zeros], axis=1)
                states = jnp.concatenate([upper, jnp.concatenate([zeros, blocks[j + 1]], axis=1)], axis=0)
            linear = jnp.dot(q_v[g, :, here], states, preferred_element_type=F32)
            for col in range(0, linear.shape[1], BLOCK):
                piece = linear[:, col : col + BLOCK]
                squares += piece * piece
            lin_v[:, here] = (linear * gain_v[g, :, here]).astype(BF16)
        ssq_v[...] = squares
        factor2 = r2_v[...]
        mean = jnp.sum(squares, axis=1, keepdims=True) / width
        scale = jnp.sqrt(factor2) * lax.rsqrt(factor2 * mean + EPSILON)
        for col in range(0, width, 2 * BLOCK):
            here = slice(col, min(col + 2 * BLOCK, width))
            done = jnp.dot(lin_v[...], wo_v[g, :, here], preferred_element_type=F32)
            total = acc_v[:, here] + done
            acc_v[:, here] = total
            for at in range(col, here.stop, BLOCK):
                piece = x_v[:, at : at + BLOCK].astype(F32) + total[:, at - col : at - col + BLOCK] * scale
                out_v[0, :, at : at + BLOCK] = piece.astype(BF16)

    for copy in gain_copies:
        copy.wait()
    x_copy.wait()
    for part in range(2):
        w_copy(1, part).start()
    total = jnp.zeros((rows, BLOCK), F32)
    for col in range(0, width, BLOCK):
        piece = x_v[:, col : col + BLOCK].astype(F32)
        total += piece * piece
        xg_v[:, col : col + BLOCK] = (piece * norm_gain[col : col + BLOCK].astype(F32)).astype(BF16)
    mean = jnp.sum(total, axis=1, keepdims=True) / width
    r2_v[...] = jnp.broadcast_to(1.0 / (mean + EPSILON), (rows, BLOCK))
    for g in range(n_groups):
        gain_v[g, 0] = out_gain[g * wide : (g + 1) * wide].astype(F32)
    ssq_v[...] = jnp.zeros_like(ssq_v)
    each_group(project)
    query()
    if comm:
        each_group(send_share)
        each_group(send_causal)
    acc_v[...] = jnp.zeros_like(acc_v)
    if comm:
        each_group(sent)
    each_group(attend)


def make_call(rows, width, comm=True):
    wide = COUNT * BLOCK
    n_groups = width // wide
    vm = pltpu.VMEM
    dma = pltpu.SemaphoreType.DMA
    each = dma((n_groups,))
    slots = vm((n_groups, PEERS * DEEP, BLOCK), F32)
    scratch = [
        vm((rows, width), BF16),
        vm((rows, width), BF16),
        vm((COUNT, BLOCK, rows), BF16),
        vm((n_groups, width, 2 * wide), BF16),
        vm((width, width), BF16),
        vm((n_groups, wide, width), BF16),
        vm((rows, 2 * wide), BF16),
        vm((n_groups, rows, wide), BF16),
        vm((rows, wide), BF16),
        vm((rows, width), F32),
        vm((rows, BLOCK), F32),
        vm((rows, BLOCK), F32),
        vm((width,), BF16), vm((width,), BF16), vm((n_groups, 1, wide), F32),
        slots, slots, vm((n_groups, DEEP, BLOCK), F32), slots, slots,
        dma, dma((2,)), dma((n_groups, 2)), dma, each,
        each, each, dma((n_groups, PEERS)), dma((n_groups, PEERS)), each, each,
    ]
    hbm = pl.BlockSpec(memory_space=pltpu.HBM)
    return pl.pallas_call(
        functools.partial(kernel, comm),
        out_shape=pltpu.VMEM((1, rows, width), BF16),
        in_specs=[hbm] * 5,
        out_specs=pl.BlockSpec(memory_space=pltpu.VMEM),
        scratch_shapes=scratch,
        compiler_params=pltpu.CompilerParams(
            collective_id=0 if comm else None, has_side_effects=comm, vmem_limit_bytes=60 * 2**20
        ),
        cost_estimate=pl.CostEstimate(flops=10**10, bytes_accessed=15 * 10**6, transcendentals=0),
    )


def body(frames_in, norm_gain, w_qkv, out_gain, w_out):
    call = make_call(frames_in.shape[1], frames_in.shape[2])
    return call(frames_in, norm_gain, w_qkv, out_gain, w_out)


def solution(mesh):
    in_specs = (P("tm", "rows", None), P(), P(), P(), P())
    out_specs = P("tm", "rows", None)
    return jax.shard_map(body, mesh=mesh, in_specs=in_specs, out_specs=out_specs, check_vma=False)
```

```python
import functools

import jax
import jax.numpy as jnp
from jax import lax
from jax.experimental import pallas as pl
from jax.experimental.pallas import tpu as pltpu
from jax.sharding import PartitionSpec as P

HEAD_DIM = 32
EPSILON = 1e-06
BLOCK = 128
COUNT = 3
DEEP = 8
PEERS = 16
SIDE = 4
F32, BF16 = jnp.float32, jnp.bfloat16
MESH = pl.DeviceIdType.MESH
AWAY = sorted(
    ((dx, dy) for dx in range(SIDE) for dy in range(SIDE) if dx or dy),
    key=lambda d: -sum(min(a, SIDE - a) for a in d),
)


def kernel(
    comm,
    x_hbm, norm_gain_hbm, wqkv_hbm, out_gain_hbm, wout_hbm, out_v,
    x_v, xg_v, kt_v, w_v, wq_v, wo_v, kv_v, q_v, lin_v, acc_v, r2_v, ssq_v, norm_gain, out_gain, gain_v,
    sends, parts, owns, shares, wholes,
    x_sem, gain_sem, w_sem, wq_sem, wo_sem, s1, r1, s2, r2, s3, r3,
):
    rows, width = x_v.shape
    n_groups, _, wide = q_v.shape
    frame, band = (lax.axis_index("tm"), lax.axis_index("rows")) if comm else (0, 0)

    first_sent = jnp.where(frame < PEERS // 2, 1, 0)
    lag = jnp.where(frame < 2, 0, 2)

    gain_copies = [
        pltpu.make_async_copy(norm_gain_hbm, norm_gain, gain_sem.at[0]),
        pltpu.make_async_copy(out_gain_hbm, out_gain, gain_sem.at[1]),
    ]
    x_copy = pltpu.make_async_copy(x_hbm.at[0], x_v, x_sem)
    for copy in gain_copies:
        copy.start()
    x_copy.start()

    def w_copy(g, part):
        src = wqkv_hbm.at[:, pl.ds(pl.multiple_of((1, 2, 0)[part] * width + g * wide, BLOCK), wide)]
        dst = w_v.at[g, :, pl.ds(part * wide, wide)] if part < 2 else wq_v.at[g]
        return pltpu.make_async_copy(src, dst, w_sem.at[g, part] if part < 2 else wq_sem.at[g])

    def wo_copy(g):
        src = wout_hbm.at[pl.ds(pl.multiple_of(g * wide, BLOCK), wide)]
        return pltpu.make_async_copy(src, wo_v.at[g], wo_sem.at[g])

    for part in range(2):
        w_copy(0, part).start()

    if comm:
        barrier = pltpu.get_barrier_semaphore()

        def greet(k, _):
            pl.semaphore_signal(barrier, inc=1, device_id={"rows": lax.rem(band + k, PEERS)}, device_id_type=MESH)
            pl.semaphore_signal(barrier, inc=1, device_id={"tm": lax.rem(frame + k, PEERS)}, device_id_type=MESH)
            return _

        lax.fori_loop(1, PEERS, greet, 0)

    others = [lax.rem(band // SIDE + dx, SIDE) * SIDE + lax.rem(band + dy, SIDE) for dx, dy in AWAY]

    def mesh_copy(src, dst, send_sem, recv_sem, where):
        return pltpu.make_async_remote_copy(
            src_ref=src, dst_ref=dst, send_sem=send_sem, recv_sem=recv_sem, device_id=where, device_id_type=MESH
        )

    def slot(buf, g, index):
        return buf.at[g, pl.ds(pl.multiple_of(index * DEEP, 8), DEEP)]

    def bulk(buf, g):
        return buf.at[g, pl.ds(0, (PEERS - 1) * DEEP)]

    def part_copies(g):
        return mesh_copy(bulk(sends, g), bulk(parts, g), s1.at[g], r1.at[g], {"rows": band})

    def share_copy(g, source, to):
        return mesh_copy(owns.at[g], slot(shares, g, source), s2.at[g, to], r2.at[g, source], {"tm": to})

    def whole_copies(g):
        return mesh_copy(bulk(wholes, g), bulk(wholes, g), s3.at[g], r3.at[g], {"rows": band})

    def send_parts(g):
        for k, to in enumerate(others):
            mesh_copy(slot(sends, g, to), slot(parts, g, k), s1.at[g], r1.at[g], {"rows": to}).start()

    def send_share(g):
        part_copies(g).wait_recv()
        total = slot(sends, g, band)[...]
        for k in range(PEERS - 1):
            total += slot(parts, g, k)[...]
        owns[g] = total

        def send(to, _):
            share_copy(g, frame, to).start()
            return _

        lax.fori_loop(frame + 1, PEERS, send, 0)

    def send_causal(g):
        def arrived(i, _):
            share_copy(g, i, i).wait_recv()
            return _

        lax.fori_loop(0, frame, arrived, 0)
        total = owns[g]
        for i in range(PEERS - 1):
            total += jnp.where(i < frame, slot(shares, g, i)[...], 0.0)
        mine = slot(wholes, g, band)
        mine[...] = total
        for to in others:
            mesh_copy(mine, mine, s3.at[g], r3.at[g], {"rows": to}).start()

    def sent(g):
        part_copies(g).wait_send()

        def gone(to, _):
            share_copy(g, frame, to).wait_send()
            return _

        lax.fori_loop(frame + 1, PEERS, gone, 0)
        whole_copies(g).wait_send()

    def each_group(step):
        def one(g, _):
            step(g)
            return _

        lax.fori_loop(0, n_groups, one, 0)

    lane_head = lax.broadcasted_iota(jnp.int32, (HEAD_DIM, BLOCK), 1) // HEAD_DIM

    def project(g):
        for part in range(2):
            w_copy(g, part).wait()

        @pl.when(g == 0)
        def _():
            for part in range(2):
                w_copy(2, part).start()

        @pl.when(g == 1)
        def _():
            for i in range(n_groups):
                w_copy(i, 2).start()

        @pl.when(g == 2)
        def _():
            for i in range(n_groups):
                wo_copy(i).start()

        for at in range(0, 2 * wide, 2 * BLOCK):
            for top in range(0, rows, 416):
                done = jnp.dot(xg_v[top : top + 416], w_v[g, :, at : at + 2 * BLOCK], preferred_element_type=F32)
                for col in range(at, at + 2 * BLOCK, BLOCK):
                    piece = done[:, col - at : col - at + BLOCK]
                    if col < wide:
                        kv_v[top : top + 416, col : col + BLOCK] = (jnp.maximum(piece, 0.0) * r2_v[top : top + 416]).astype(BF16)
                    else:
                        kv_v[top : top + 416, col : col + BLOCK] = piece.astype(BF16)
            if at + 2 * BLOCK <= wide + BLOCK:
                for j in range(at // BLOCK, min(at // BLOCK + 2, COUNT)):
                    kt_v[j] = kv_v[:, j * BLOCK : (j + 1) * BLOCK].T
        for j in range(COUNT):
            block = jnp.dot(kt_v[j], kv_v[:, wide + j * BLOCK : wide + (j + 1) * BLOCK], preferred_element_type=F32)
            state = jnp.where(lane_head == 0, block[:HEAD_DIM], 0.0)
            for a in range(1, BLOCK // HEAD_DIM):
                state += jnp.where(lane_head == a, block[a * HEAD_DIM : (a + 1) * HEAD_DIM], 0.0)
            for half in range(2):
                sends[g, pl.ds(2 * j + half, PEERS, stride=DEEP), :] = state[half * PEERS : (half + 1) * PEERS]
        if comm:

            @pl.when(g == first_sent)
            def _():
                pl.semaphore_wait(barrier, 2 * (PEERS - 1))

            @pl.when(jnp.logical_and(g == 1, first_sent == 1))
            def _():
                send_parts(0)

            @pl.when(g >= first_sent)
            def _():
                send_parts(g)

    def query(g):
        w_copy(g, 2).wait()
        done = jnp.dot(xg_v[...], wq_v[g], preferred_element_type=F32)
        q_v[g] = jnp.maximum(done, 0.0).astype(BF16)

    def exchange(step, carry):
        @pl.when(step < n_groups)
        def _():
            query(step)
            send_share(step)

        @pl.when(step >= lag)
        def _():
            send_causal(step - lag)

        return carry

    def attend(g):
        wo_copy(g).wait()
        if comm:
            whole_copies(g).wait_recv()
        whole = wholes if comm else sends
        blocks = []
        for j in range(COUNT):
            state = jnp.concatenate([whole[g, pl.ds(2 * j + half, PEERS, stride=DEEP), :] for half in range(2)], axis=0)
            heads = [jnp.where(lane_head == a, state, 0.0) for a in range(BLOCK // HEAD_DIM)]
            blocks.append(jnp.concatenate(heads, axis=0).astype(BF16))
        zeros = jnp.zeros((BLOCK, BLOCK), BF16)
        squares = ssq_v[...]
        for j in range(0, COUNT, 2):
            here = slice(j * BLOCK, min(j + 2, COUNT) * BLOCK)
            states = blocks[j]
            if j + 1 < COUNT:
                upper = jnp.concatenate([states, zeros], axis=1)
                states = jnp.concatenate([upper, jnp.concatenate([zeros, blocks[j + 1]], axis=1)], axis=0)
            linear = jnp.dot(q_v[g, :, here], states, preferred_element_type=F32)
            for col in range(0, linear.shape[1], BLOCK):
                piece = linear[:, col : col + BLOCK]
                squares += piece * piece
            lin_v[:, here] = (linear * gain_v[g, :, here]).astype(BF16)
        ssq_v[...] = squares
        factor2 = r2_v[...]
        mean = jnp.sum(squares, axis=1, keepdims=True) / width
        scale = jnp.sqrt(factor2) * lax.rsqrt(factor2 * mean + EPSILON)
        for col in range(0, width, 2 * BLOCK):
            here = slice(col, min(col + 2 * BLOCK, width))
            done = jnp.dot(lin_v[...], wo_v[g, :, here], preferred_element_type=F32)
            total = acc_v[:, here] + done
            acc_v[:, here] = total
            for at in range(col, here.stop, BLOCK):
                piece = x_v[:, at : at + BLOCK].astype(F32) + total[:, at - col : at - col + BLOCK] * scale
                out_v[0, :, at : at + BLOCK] = piece.astype(BF16)

    for copy in gain_copies:
        copy.wait()
    x_copy.wait()
    for part in range(2):
        w_copy(1, part).start()
    total = jnp.zeros((rows, BLOCK), F32)
    for col in range(0, width, BLOCK):
        piece = x_v[:, col : col + BLOCK].astype(F32)
        total += piece * piece
        xg_v[:, col : col + BLOCK] = (piece * norm_gain[col : col + BLOCK].astype(F32)).astype(BF16)
    mean = jnp.sum(total, axis=1, keepdims=True) / width
    r2_v[...] = jnp.broadcast_to(1.0 / (mean + EPSILON), (rows, BLOCK))
    for g in range(n_groups):
        gain_v[g, 0] = out_gain[g * wide : (g + 1) * wide].astype(F32)
    ssq_v[...] = jnp.zeros_like(ssq_v)
    each_group(project)
    if comm:
        lax.fori_loop(0, n_groups + lag, exchange, 0)
    else:
        each_group(query)
    acc_v[...] = jnp.zeros_like(acc_v)
    if comm:
        each_group(sent)
    each_group(attend)


def make_call(rows, width, comm=True):
    wide = COUNT * BLOCK
    n_groups = width // wide
    vm = pltpu.VMEM
    dma = pltpu.SemaphoreType.DMA
    each = dma((n_groups,))
    slots = vm((n_groups, PEERS * DEEP, BLOCK), F32)
    scratch = [
        vm((rows, width), BF16),
        vm((rows, width), BF16),
        vm((COUNT, BLOCK, rows), BF16),
        vm((n_groups, width, 2 * wide), BF16),
        vm((n_groups, width, wide), BF16),
        vm((n_groups, wide, width), BF16),
        vm((rows, 2 * wide), BF16),
        vm((n_groups, rows, wide), BF16),
        vm((rows, wide), BF16),
        vm((rows, width), F32),
        vm((rows, BLOCK), F32),
        vm((rows, BLOCK), F32),
        vm((width,), BF16), vm((width,), BF16), vm((n_groups, 1, wide), F32),
        slots, slots, vm((n_groups, DEEP, BLOCK), F32), slots, slots,
        dma, dma((2,)), dma((n_groups, 2)), each, each,
        each, each, dma((n_groups, PEERS)), dma((n_groups, PEERS)), each, each,
    ]
    hbm = pl.BlockSpec(memory_space=pltpu.HBM)
    return pl.pallas_call(
        functools.partial(kernel, comm),
        out_shape=pltpu.VMEM((1, rows, width), BF16),
        in_specs=[hbm] * 5,
        out_specs=pl.BlockSpec(memory_space=pltpu.VMEM),
        scratch_shapes=scratch,
        compiler_params=pltpu.CompilerParams(
            collective_id=0 if comm else None, has_side_effects=comm, vmem_limit_bytes=60 * 2**20
        ),
        cost_estimate=pl.CostEstimate(flops=10**10, bytes_accessed=15 * 10**6, transcendentals=0),
    )


def body(frames_in, norm_gain, w_qkv, out_gain, w_out):
    call = make_call(frames_in.shape[1], frames_in.shape[2])
    return call(frames_in, norm_gain, w_qkv, out_gain, w_out)


def solution(mesh):
    in_specs = (P("tm", "rows", None), P(), P(), P(), P())
    out_specs = P("tm", "rows", None)
    return jax.shard_map(body, mesh=mesh, in_specs=in_specs, out_specs=out_specs, check_vma=False)
```

```python
import functools

import jax
import jax.numpy as jnp
from jax import lax
from jax.experimental import pallas as pl
from jax.experimental.pallas import tpu as pltpu
from jax.sharding import PartitionSpec as P

HEAD_DIM = 32
EPSILON = 1e-06
BLOCK = 128
COUNT = 3
DEEP = 8
PEERS = 16
SIDE = 4
F32, BF16 = jnp.float32, jnp.bfloat16
MESH = pl.DeviceIdType.MESH
AWAY = sorted(
    ((dx, dy) for dx in range(SIDE) for dy in range(SIDE) if dx or dy),
    key=lambda d: -sum(min(a, SIDE - a) for a in d),
)


def kernel(
    comm,
    x_hbm, norm_gain_hbm, wqkv_hbm, out_gain_hbm, wout_hbm, out_v,
    x_v, xg_v, kt_v, w_v, wq_v, wo_v, kv_v, q_v, lin_v, acc_v, r2_v, ssq_v, norm_gain, out_gain, gain_v,
    sends, parts, owns, shares, wholes,
    x_sem, gain_sem, w_sem, wq_sem, wo_sem, s1, r1, s2, r2, s3, r3,
):
    rows, width = x_v.shape
    n_groups, _, wide = q_v.shape
    frame, band = (lax.axis_index("tm"), lax.axis_index("rows")) if comm else (0, 0)

    first_sent = jnp.where(frame < PEERS // 2, 1, 0)
    lag = jnp.where(frame < 2, 0, 2)

    gain_copies = [
        pltpu.make_async_copy(norm_gain_hbm, norm_gain, gain_sem.at[0]),
        pltpu.make_async_copy(out_gain_hbm, out_gain, gain_sem.at[1]),
    ]
    x_copy = pltpu.make_async_copy(x_hbm.at[0], x_v, x_sem)
    for copy in gain_copies:
        copy.start()
    x_copy.start()

    def w_copy(g, part):
        src = wqkv_hbm.at[:, pl.ds(pl.multiple_of((1, 2, 0)[part] * width + g * wide, BLOCK), wide)]
        dst = w_v.at[g, :, pl.ds(part * wide, wide)] if part < 2 else wq_v.at[g]
        return pltpu.make_async_copy(src, dst, w_sem.at[g, part] if part < 2 else wq_sem.at[g])

    def wo_copy(g):
        src = wout_hbm.at[pl.ds(pl.multiple_of(g * wide, BLOCK), wide)]
        return pltpu.make_async_copy(src, wo_v.at[g], wo_sem.at[g])

    for part in range(2):
        w_copy(0, part).start()

    if comm:
        barrier = pltpu.get_barrier_semaphore()

        def greet(k, _):
            pl.semaphore_signal(barrier, inc=1, device_id={"rows": lax.rem(band + k, PEERS)}, device_id_type=MESH)
            pl.semaphore_signal(barrier, inc=1, device_id={"tm": lax.rem(frame + k, PEERS)}, device_id_type=MESH)
            return _

        lax.fori_loop(1, PEERS, greet, 0)

    others = [lax.rem(band // SIDE + dx, SIDE) * SIDE + lax.rem(band + dy, SIDE) for dx, dy in AWAY]

    def mesh_copy(src, dst, send_sem, recv_sem, where):
        return pltpu.make_async_remote_copy(
            src_ref=src, dst_ref=dst, send_sem=send_sem, recv_sem=recv_sem, device_id=where, device_id_type=MESH
        )

    def slot(buf, g, index):
        return buf.at[g, pl.ds(pl.multiple_of(index * DEEP, 8), DEEP)]

    def bulk(buf, g):
        return buf.at[g, pl.ds(0, (PEERS - 1) * DEEP)]

    def part_copies(g):
        return mesh_copy(bulk(sends, g), bulk(parts, g), s1.at[g], r1.at[g], {"rows": band})

    def share_copy(g, source, to):
        return mesh_copy(owns.at[g], slot(shares, g, source), s2.at[g, to], r2.at[g, source], {"tm": to})

    def whole_copies(g):
        return mesh_copy(bulk(wholes, g), bulk(wholes, g), s3.at[g], r3.at[g], {"rows": band})

    def send_parts(g):
        for k, to in enumerate(others):
            mesh_copy(slot(sends, g, to), slot(parts, g, k), s1.at[g], r1.at[g], {"rows": to}).start()

    def send_share(g):
        part_copies(g).wait_recv()
        total = slot(sends, g, band)[...]
        for k in range(PEERS - 1):
            total += slot(parts, g, k)[...]
        owns[g] = total

        def send(i, _):
            share_copy(g, frame, PEERS - 1 - i).start()
            return _

        lax.fori_loop(0, PEERS - 1 - frame, send, 0)

    def send_causal(g):
        def arrived(i, _):
            share_copy(g, i, i).wait_recv()
            return _

        lax.fori_loop(0, frame, arrived, 0)
        total = owns[g]
        for i in range(PEERS - 1):
            total += jnp.where(i < frame, slot(shares, g, i)[...], 0.0)
        mine = slot(wholes, g, band)
        mine[...] = total
        for to in others:
            mesh_copy(mine, mine, s3.at[g], r3.at[g], {"rows": to}).start()

    def sent(g):
        part_copies(g).wait_send()

        def gone(to, _):
            share_copy(g, frame, to).wait_send()
            return _

        lax.fori_loop(frame + 1, PEERS, gone, 0)
        whole_copies(g).wait_send()

    def each_group(step):
        def one(g, _):
            step(g)
            return _

        lax.fori_loop(0, n_groups, one, 0)

    lane_head = lax.broadcasted_iota(jnp.int32, (HEAD_DIM, BLOCK), 1) // HEAD_DIM

    def project(g):
        for part in range(2):
            w_copy(g, part).wait()

        @pl.when(g == 0)
        def _():
            for part in range(2):
                w_copy(2, part).start()

        @pl.when(g == 1)
        def _():
            for i in range(n_groups):
                w_copy(i, 2).start()

        @pl.when(g == 2)
        def _():
            for i in range(n_groups):
                wo_copy(i).start()

        for at in range(0, 2 * wide, 2 * BLOCK):
            for top in range(0, rows, 416):
                done = jnp.dot(xg_v[top : top + 416], w_v[g, :, at : at + 2 * BLOCK], preferred_element_type=F32)
                for col in range(at, at + 2 * BLOCK, BLOCK):
                    piece = done[:, col - at : col - at + BLOCK]
                    if col < wide:
                        kv_v[top : top + 416, col : col + BLOCK] = (jnp.maximum(piece, 0.0) * r2_v[top : top + 416]).astype(BF16)
                    else:
                        kv_v[top : top + 416, col : col + BLOCK] = piece.astype(BF16)
            if at + 2 * BLOCK <= wide + BLOCK:
                for j in range(at // BLOCK, min(at // BLOCK + 2, COUNT)):
                    kt_v[j] = kv_v[:, j * BLOCK : (j + 1) * BLOCK].T
        for j in range(COUNT):
            block = jnp.dot(kt_v[j], kv_v[:, wide + j * BLOCK : wide + (j + 1) * BLOCK], preferred_element_type=F32)
            state = jnp.where(lane_head == 0, block[:HEAD_DIM], 0.0)
            for a in range(1, BLOCK // HEAD_DIM):
                state += jnp.where(lane_head == a, block[a * HEAD_DIM : (a + 1) * HEAD_DIM], 0.0)
            for half in range(2):
                sends[g, pl.ds(2 * j + half, PEERS, stride=DEEP), :] = state[half * PEERS : (half + 1) * PEERS]
        if comm:

            @pl.when(g == first_sent)
            def _():
                pl.semaphore_wait(barrier, 2 * (PEERS - 1))

            @pl.when(jnp.logical_and(g == 1, first_sent == 1))
            def _():
                send_parts(0)

            @pl.when(g >= first_sent)
            def _():
                send_parts(g)

    def query(g):
        w_copy(g, 2).wait()
        done = jnp.dot(xg_v[...], wq_v[g], preferred_element_type=F32)
        q_v[g] = jnp.maximum(done, 0.0).astype(BF16)

    def exchange(step, carry):
        @pl.when(jnp.logical_or(step < n_groups - 1, step == n_groups))
        def _():
            query(jnp.minimum(step, n_groups - 1))

        @pl.when(step < n_groups)
        def _():
            send_share(step)

        @pl.when(jnp.logical_and(step >= lag, step < n_groups + lag))
        def _():
            send_causal(step - lag)

        return carry

    def attend(g):
        wo_copy(g).wait()
        if comm:
            whole_copies(g).wait_recv()
        whole = wholes if comm else sends
        blocks = []
        for j in range(COUNT):
            state = jnp.concatenate([whole[g, pl.ds(2 * j + half, PEERS, stride=DEEP), :] for half in range(2)], axis=0)
            heads = [jnp.where(lane_head == a, state, 0.0) for a in range(BLOCK // HEAD_DIM)]
            blocks.append(jnp.concatenate(heads, axis=0).astype(BF16))
        zeros = jnp.zeros((BLOCK, BLOCK), BF16)
        squares = ssq_v[...]
        for j in range(0, COUNT, 2):
            here = slice(j * BLOCK, min(j + 2, COUNT) * BLOCK)
            states = blocks[j]
            if j + 1 < COUNT:
                upper = jnp.concatenate([states, zeros], axis=1)
                states = jnp.concatenate([upper, jnp.concatenate([zeros, blocks[j + 1]], axis=1)], axis=0)
            linear = jnp.dot(q_v[g, :, here], states, preferred_element_type=F32)
            for col in range(0, linear.shape[1], BLOCK):
                piece = linear[:, col : col + BLOCK]
                squares += piece * piece
            lin_v[:, here] = (linear * gain_v[g, :, here]).astype(BF16)
        ssq_v[...] = squares
        factor2 = r2_v[...]
        mean = jnp.sum(squares, axis=1, keepdims=True) / width
        scale = jnp.sqrt(factor2) * lax.rsqrt(factor2 * mean + EPSILON)
        for col in range(0, width, 2 * BLOCK):
            here = slice(col, min(col + 2 * BLOCK, width))
            done = jnp.dot(lin_v[...], wo_v[g, :, here], preferred_element_type=F32)
            total = acc_v[:, here] + done
            acc_v[:, here] = total
            for at in range(col, here.stop, BLOCK):
                piece = x_v[:, at : at + BLOCK].astype(F32) + total[:, at - col : at - col + BLOCK] * scale
                out_v[0, :, at : at + BLOCK] = piece.astype(BF16)

    for copy in gain_copies:
        copy.wait()
    x_copy.wait()
    for part in range(2):
        w_copy(1, part).start()
    total = jnp.zeros((rows, BLOCK), F32)
    for col in range(0, width, BLOCK):
        piece = x_v[:, col : col + BLOCK].astype(F32)
        total += piece * piece
        xg_v[:, col : col + BLOCK] = (piece * norm_gain[col : col + BLOCK].astype(F32)).astype(BF16)
    mean = jnp.sum(total, axis=1, keepdims=True) / width
    r2_v[...] = jnp.broadcast_to(1.0 / (mean + EPSILON), (rows, BLOCK))
    for g in range(n_groups):
        gain_v[g, 0] = out_gain[g * wide : (g + 1) * wide].astype(F32)
    ssq_v[...] = jnp.zeros_like(ssq_v)
    each_group(project)
    if comm:
        lax.fori_loop(0, n_groups + jnp.maximum(lag, 1), exchange, 0)
    else:
        each_group(query)
    acc_v[...] = jnp.zeros_like(acc_v)
    if comm:
        each_group(sent)
    each_group(attend)


def make_call(rows, width, comm=True):
    wide = COUNT * BLOCK
    n_groups = width // wide
    vm = pltpu.VMEM
    dma = pltpu.SemaphoreType.DMA
    each = dma((n_groups,))
    slots = vm((n_groups, PEERS * DEEP, BLOCK), F32)
    scratch = [
        vm((rows, width), BF16),
        vm((rows, width), BF16),
        vm((COUNT, BLOCK, rows), BF16),
        vm((n_groups, width, 2 * wide), BF16),
        vm((n_groups, width, wide), BF16),
        vm((n_groups, wide, width), BF16),
        vm((rows, 2 * wide), BF16),
        vm((n_groups, rows, wide), BF16),
        vm((rows, wide), BF16),
        vm((rows, width), F32),
        vm((rows, BLOCK), F32),
        vm((rows, BLOCK), F32),
        vm((width,), BF16), vm((width,), BF16), vm((n_groups, 1, wide), F32),
        slots, slots, vm((n_groups, DEEP, BLOCK), F32), slots, slots,
        dma, dma((2,)), dma((n_groups, 2)), each, each,
        each, each, dma((n_groups, PEERS)), dma((n_groups, PEERS)), each, each,
    ]
    hbm = pl.BlockSpec(memory_space=pltpu.HBM)
    return pl.pallas_call(
        functools.partial(kernel, comm),
        out_shape=pltpu.VMEM((1, rows, width), BF16),
        in_specs=[hbm] * 5,
        out_specs=pl.BlockSpec(memory_space=pltpu.VMEM),
        scratch_shapes=scratch,
        compiler_params=pltpu.CompilerParams(
            collective_id=0 if comm else None, has_side_effects=comm, vmem_limit_bytes=60 * 2**20
        ),
        cost_estimate=pl.CostEstimate(flops=10**10, bytes_accessed=15 * 10**6, transcendentals=0),
    )


def body(frames_in, norm_gain, w_qkv, out_gain, w_out):
    call = make_call(frames_in.shape[1], frames_in.shape[2])
    return call(frames_in, norm_gain, w_qkv, out_gain, w_out)


def solution(mesh):
    in_specs = (P("tm", "rows", None), P(), P(), P(), P())
    out_specs = P("tm", "rows", None)
    return jax.shard_map(body, mesh=mesh, in_specs=in_specs, out_specs=out_specs, check_vma=False)
```

```python
import functools

import jax
import jax.numpy as jnp
from jax import lax
from jax.experimental import pallas as pl
from jax.experimental.pallas import tpu as pltpu
from jax.sharding import PartitionSpec as P

HEAD_DIM = 32
EPSILON = 1e-06
BLOCK = 128
COUNT = 3
DEEP = 8
PEERS = 16
SIDE = 4
F32, BF16 = jnp.float32, jnp.bfloat16
MESH = pl.DeviceIdType.MESH
AWAY = sorted(
    ((dx, dy) for dx in range(SIDE) for dy in range(SIDE) if dx or dy),
    key=lambda d: -sum(min(a, SIDE - a) for a in d),
)


def kernel(
    comm,
    x_hbm, norm_gain_hbm, wqkv_hbm, out_gain_hbm, wout_hbm, out_v,
    x_v, xg_v, kt_v, w_v, wq_v, wo_v, kv_v, q_v, lin_v, acc_v, r2_v, ssq_v, norm_gain, out_gain, gain_v,
    sends, parts, owns, shares, wholes,
    x_sem, gain_sem, w_sem, wq_sem, wo_sem, s1, r1, s2, r2, s3, r3,
):
    rows, width = x_v.shape
    n_groups, _, wide = q_v.shape
    frame, band = (lax.axis_index("tm"), lax.axis_index("rows")) if comm else (0, 0)

    first_sent = jnp.where(frame < PEERS // 2, 1, 0)
    lag = jnp.where(frame < 2, 0, 2)
    skipped = jnp.where(frame < PEERS // 2, n_groups - 1, 0)

    gain_copies = [
        pltpu.make_async_copy(norm_gain_hbm, norm_gain, gain_sem.at[0]),
        pltpu.make_async_copy(out_gain_hbm, out_gain, gain_sem.at[1]),
    ]
    x_copy = pltpu.make_async_copy(x_hbm.at[0], x_v, x_sem)
    for copy in gain_copies:
        copy.start()
    x_copy.start()

    def w_copy(g, part):
        src = wqkv_hbm.at[:, pl.ds(pl.multiple_of((1, 2, 0)[part] * width + g * wide, BLOCK), wide)]
        dst = w_v.at[g, :, pl.ds(part * wide, wide)] if part < 2 else wq_v.at[g]
        return pltpu.make_async_copy(src, dst, w_sem.at[g, part] if part < 2 else wq_sem.at[g])

    def wo_copy(g):
        src = wout_hbm.at[pl.ds(pl.multiple_of(g * wide, BLOCK), wide)]
        return pltpu.make_async_copy(src, wo_v.at[g], wo_sem.at[g])

    for part in range(2):
        w_copy(0, part).start()

    if comm:
        barrier = pltpu.get_barrier_semaphore()

        def greet(k, _):
            pl.semaphore_signal(barrier, inc=1, device_id={"rows": lax.rem(band + k, PEERS)}, device_id_type=MESH)
            pl.semaphore_signal(barrier, inc=1, device_id={"tm": lax.rem(frame + k, PEERS)}, device_id_type=MESH)
            return _

        lax.fori_loop(1, PEERS, greet, 0)

    others = [lax.rem(band // SIDE + dx, SIDE) * SIDE + lax.rem(band + dy, SIDE) for dx, dy in AWAY]

    def mesh_copy(src, dst, send_sem, recv_sem, where):
        return pltpu.make_async_remote_copy(
            src_ref=src, dst_ref=dst, send_sem=send_sem, recv_sem=recv_sem, device_id=where, device_id_type=MESH
        )

    def slot(buf, g, index):
        return buf.at[g, pl.ds(pl.multiple_of(index * DEEP, 8), DEEP)]

    def bulk(buf, g):
        return buf.at[g, pl.ds(0, (PEERS - 1) * DEEP)]

    def part_copies(g):
        return mesh_copy(bulk(sends, g), bulk(parts, g), s1.at[g], r1.at[g], {"rows": band})

    def share_copy(g, source, to):
        return mesh_copy(owns.at[g], slot(shares, g, source), s2.at[g, to], r2.at[g, source], {"tm": to})

    def whole_copies(g):
        return mesh_copy(bulk(wholes, g), bulk(wholes, g), s3.at[g], r3.at[g], {"rows": band})

    def send_parts(g):
        for k, to in enumerate(others):
            mesh_copy(slot(sends, g, to), slot(parts, g, k), s1.at[g], r1.at[g], {"rows": to}).start()

    def send_share(g):
        part_copies(g).wait_recv()
        total = slot(sends, g, band)[...]
        for k in range(PEERS - 1):
            total += slot(parts, g, k)[...]
        owns[g] = total

        def send(i, _):
            share_copy(g, frame, PEERS - 1 - i).start()
            return _

        lax.fori_loop(0, PEERS - 1 - frame, send, 0)

    def send_causal(g):
        def arrived(i, _):
            share_copy(g, i, i).wait_recv()
            return _

        lax.fori_loop(0, frame, arrived, 0)
        total = owns[g]
        for i in range(PEERS - 1):
            total += jnp.where(i < frame, slot(shares, g, i)[...], 0.0)
        mine = slot(wholes, g, band)
        mine[...] = total
        for to in others:
            mesh_copy(mine, mine, s3.at[g], r3.at[g], {"rows": to}).start()

    def sent(g):
        part_copies(g).wait_send()

        def gone(to, _):
            share_copy(g, frame, to).wait_send()
            return _

        lax.fori_loop(frame + 1, PEERS, gone, 0)
        whole_copies(g).wait_send()

    def each_group(step):
        def one(g, _):
            step(g)
            return _

        lax.fori_loop(0, n_groups, one, 0)

    lane_head = lax.broadcasted_iota(jnp.int32, (HEAD_DIM, BLOCK), 1) // HEAD_DIM

    def project(g):
        for part in range(2):
            w_copy(g, part).wait()

        @pl.when(g == 0)
        def _():
            for part in range(2):
                w_copy(2, part).start()

        @pl.when(g == 1)
        def _():
            for i in range(n_groups):
                w_copy(i, 2).start()

        @pl.when(g == 2)
        def _():
            for i in range(n_groups):
                wo_copy(i).start()

        for at in range(0, 2 * wide, 2 * BLOCK):
            for top in range(0, rows, 416):
                done = jnp.dot(xg_v[top : top + 416], w_v[g, :, at : at + 2 * BLOCK], preferred_element_type=F32)
                for col in range(at, at + 2 * BLOCK, BLOCK):
                    piece = done[:, col - at : col - at + BLOCK]
                    if col < wide:
                        kv_v[top : top + 416, col : col + BLOCK] = (jnp.maximum(piece, 0.0) * r2_v[top : top + 416]).astype(BF16)
                    else:
                        kv_v[top : top + 416, col : col + BLOCK] = piece.astype(BF16)
            if at + 2 * BLOCK <= wide + BLOCK:
                for j in range(at // BLOCK, min(at // BLOCK + 2, COUNT)):
                    kt_v[j] = kv_v[:, j * BLOCK : (j + 1) * BLOCK].T
        for j in range(COUNT):
            block = jnp.dot(kt_v[j], kv_v[:, wide + j * BLOCK : wide + (j + 1) * BLOCK], preferred_element_type=F32)
            state = jnp.where(lane_head == 0, block[:HEAD_DIM], 0.0)
            for a in range(1, BLOCK // HEAD_DIM):
                state += jnp.where(lane_head == a, block[a * HEAD_DIM : (a + 1) * HEAD_DIM], 0.0)
            for half in range(2):
                sends[g, pl.ds(2 * j + half, PEERS, stride=DEEP), :] = state[half * PEERS : (half + 1) * PEERS]
        if comm:

            @pl.when(g == first_sent)
            def _():
                pl.semaphore_wait(barrier, 2 * (PEERS - 1))

            @pl.when(jnp.logical_and(g == 1, first_sent == 1))
            def _():
                send_parts(0)

            @pl.when(g >= first_sent)
            def _():
                send_parts(g)

    def query(g):
        w_copy(g, 2).wait()
        done = jnp.dot(xg_v[...], wq_v[g], preferred_element_type=F32)
        q_v[g] = jnp.maximum(done, 0.0).astype(BF16)

    def exchange(step, carry):
        @pl.when(jnp.logical_and(step <= n_groups, step != skipped))
        def _():
            query(step - jnp.where(step > skipped, 1, 0))

        @pl.when(step < n_groups)
        def _():
            send_share(step)

        @pl.when(jnp.logical_and(step >= lag, step < n_groups + lag))
        def _():
            send_causal(step - lag)

        return carry

    def attend(g):
        wo_copy(g).wait()
        if comm:
            whole_copies(g).wait_recv()
        whole = wholes if comm else sends
        blocks = []
        for j in range(COUNT):
            state = jnp.concatenate([whole[g, pl.ds(2 * j + half, PEERS, stride=DEEP), :] for half in range(2)], axis=0)
            heads = [jnp.where(lane_head == a, state, 0.0) for a in range(BLOCK // HEAD_DIM)]
            blocks.append(jnp.concatenate(heads, axis=0).astype(BF16))
        zeros = jnp.zeros((BLOCK, BLOCK), BF16)
        squares = ssq_v[...]
        for j in range(0, COUNT, 2):
            here = slice(j * BLOCK, min(j + 2, COUNT) * BLOCK)
            states = blocks[j]
            if j + 1 < COUNT:
                upper = jnp.concatenate([states, zeros], axis=1)
                states = jnp.concatenate([upper, jnp.concatenate([zeros, blocks[j + 1]], axis=1)], axis=0)
            linear = jnp.dot(q_v[g, :, here], states, preferred_element_type=F32)
            for col in range(0, linear.shape[1], BLOCK):
                piece = linear[:, col : col + BLOCK]
                squares += piece * piece
            lin_v[:, here] = (linear * gain_v[g, :, here]).astype(BF16)
        ssq_v[...] = squares
        factor2 = r2_v[...]
        mean = jnp.sum(squares, axis=1, keepdims=True) / width
        scale = jnp.sqrt(factor2) * lax.rsqrt(factor2 * mean + EPSILON)
        for col in range(0, width, 2 * BLOCK):
            here = slice(col, min(col + 2 * BLOCK, width))
            done = jnp.dot(lin_v[...], wo_v[g, :, here], preferred_element_type=F32)
            total = acc_v[:, here] + done
            acc_v[:, here] = total
            for at in range(col, here.stop, BLOCK):
                piece = x_v[:, at : at + BLOCK].astype(F32) + total[:, at - col : at - col + BLOCK] * scale
                out_v[0, :, at : at + BLOCK] = piece.astype(BF16)

    for copy in gain_copies:
        copy.wait()
    x_copy.wait()
    for part in range(2):
        w_copy(1, part).start()
    total = jnp.zeros((rows, BLOCK), F32)
    for col in range(0, width, BLOCK):
        piece = x_v[:, col : col + BLOCK].astype(F32)
        total += piece * piece
        xg_v[:, col : col + BLOCK] = (piece * norm_gain[col : col + BLOCK].astype(F32)).astype(BF16)
    mean = jnp.sum(total, axis=1, keepdims=True) / width
    r2_v[...] = jnp.broadcast_to(1.0 / (mean + EPSILON), (rows, BLOCK))
    for g in range(n_groups):
        gain_v[g, 0] = out_gain[g * wide : (g + 1) * wide].astype(F32)
    ssq_v[...] = jnp.zeros_like(ssq_v)
    each_group(project)
    if comm:
        lax.fori_loop(0, n_groups + jnp.maximum(lag, 1), exchange, 0)
    else:
        each_group(query)
    acc_v[...] = jnp.zeros_like(acc_v)
    if comm:
        each_group(sent)
    each_group(attend)


def make_call(rows, width, comm=True):
    wide = COUNT * BLOCK
    n_groups = width // wide
    vm = pltpu.VMEM
    dma = pltpu.SemaphoreType.DMA
    each = dma((n_groups,))
    slots = vm((n_groups, PEERS * DEEP, BLOCK), F32)
    scratch = [
        vm((rows, width), BF16),
        vm((rows, width), BF16),
        vm((COUNT, BLOCK, rows), BF16),
        vm((n_groups, width, 2 * wide), BF16),
        vm((n_groups, width, wide), BF16),
        vm((n_groups, wide, width), BF16),
        vm((rows, 2 * wide), BF16),
        vm((n_groups, rows, wide), BF16),
        vm((rows, wide), BF16),
        vm((rows, width), F32),
        vm((rows, BLOCK), F32),
        vm((rows, BLOCK), F32),
        vm((width,), BF16), vm((width,), BF16), vm((n_groups, 1, wide), F32),
        slots, slots, vm((n_groups, DEEP, BLOCK), F32), slots, slots,
        dma, dma((2,)), dma((n_groups, 2)), each, each,
        each, each, dma((n_groups, PEERS)), dma((n_groups, PEERS)), each, each,
    ]
    hbm = pl.BlockSpec(memory_space=pltpu.HBM)
    return pl.pallas_call(
        functools.partial(kernel, comm),
        out_shape=pltpu.VMEM((1, rows, width), BF16),
        in_specs=[hbm] * 5,
        out_specs=pl.BlockSpec(memory_space=pltpu.VMEM),
        scratch_shapes=scratch,
        compiler_params=pltpu.CompilerParams(
            collective_id=0 if comm else None, has_side_effects=comm, vmem_limit_bytes=60 * 2**20
        ),
        cost_estimate=pl.CostEstimate(flops=10**10, bytes_accessed=15 * 10**6, transcendentals=0),
    )


def body(frames_in, norm_gain, w_qkv, out_gain, w_out):
    call = make_call(frames_in.shape[1], frames_in.shape[2])
    return call(frames_in, norm_gain, w_qkv, out_gain, w_out)


def solution(mesh):
    in_specs = (P("tm", "rows", None), P(), P(), P(), P())
    out_specs = P("tm", "rows", None)
    return jax.shard_map(body, mesh=mesh, in_specs=in_specs, out_specs=out_specs, check_vma=False)
```
